32 devices in a mesh: gx: 2 (over y), gy: 4 (over x, core), gz: 4 (over z).
Axes of the slice: x: 2, y: 2, z: 4, core: 2. Of those that a mesh axis runs over, the one named last changes fastest.
Arguments:
- bricks: bfloat16 [256, 2, 128, 128], P(('gx', 'gy', 'gz')), may hold values from -6 to 6
- live: int32 [256], P(('gx', 'gy', 'gz')), may hold values from 1 to 2, as said below
- shear: float32 [4, 2], replicated, may hold values from -1 to 1
- offsets: int32 [256, 4, 2], P(('gx', 'gy', 'gz')), may hold values from -8 to 8
- absorb: bfloat16 [256], P(('gx', 'gy', 'gz')), may hold values from 0.019897461 to 0.119628906
- color_gain: float32 [3], replicated, may hold values from 0.5 to 3
- color_bias: float32 [3], replicated, may hold values from -1 to 1
- targets: int32 [256, 4], P(('gx', 'gy', 'gz')), may hold values from 0 to 63, as said below
- order: int32 [4, 256], P(None, ('gx', 'gy', 'gz')), may hold values from 0 to 255, each once within a row
Outputs:
- image: float32 [64, 4, 128, 128], P(('gx', 'gy', 'gz'))
The draws below stay inside these ranges and needn't reach their ends.
Inputs may be any that keep to these rules, and one draw needn't show every extreme that they name: Slices from live[b] on are empty; a device's rendering load can be up to twice another's. targets[b, v] = u has u mod 4 = v; tile u is owned by device u // 2 (devices counted in mesh order) and brick b by device b // 8, and both devices have the same gx index. A device sends at most 2 footprints to any one device; for each gx index some device receives 2 footprints from every device with that gx index. order[v] is a permutation of the bricks.
All inputs are finite; a program needn't handle non-finite values.
Results may differ from the reference program's by a relative error of at most 0.0016.
Values may be sent and summed in bfloat16 or wider, within the bound.
A program may use at most 64 MiB of HBM per device.

```python
import math
import jax
import jax.numpy as jnp
from jax import lax

FOOT = 128
DEPTH = 2
BRICK_DEV = 8
VIEWS = 4
ROW = 16
CAP = 2
BRICKS = 256
TILES = 64


def draw_live(key, part):
    devices_all = BRICKS // BRICK_DEV
    ceiling = jax.random.randint(jax.random.fold_in(key, 11), (devices_all, 1), 1, DEPTH + 1)
    uniform_bits = jax.random.randint(jax.random.fold_in(key, 12), (devices_all, BRICK_DEV), 0, 1 << 20)
    counts_live = 1 + uniform_bits % ceiling
    chosen_brick = jax.random.randint(jax.random.fold_in(key, 13), (), 0, BRICKS)
    return counts_live.reshape(BRICKS).at[chosen_brick].set(DEPTH).astype(jnp.int32)


def draw_targets(key, part):
    groups_all = BRICKS // BRICK_DEV // ROW
    slot_span = ROW // 2 * CAP
    pick_count = 2 * BRICK_DEV
    slot_index = jnp.arange(slot_span)
    slot_owner = slot_index // CAP
    noise_bits = jax.random.randint(jax.random.fold_in(key, 21), (groups_all, ROW, 2, slot_span), 0, 1 << 20)
    busiest = jax.random.randint(jax.random.fold_in(key, 22), (groups_all, 1, 2, 1), 0, ROW // 2)
    scores = jnp.where(slot_owner == busiest, slot_index - slot_span, noise_bits * slot_span + slot_index)
    picked = jnp.argsort(scores, axis=-1)[..., :pick_count]
    mixing = jax.random.randint(jax.random.fold_in(key, 23), (groups_all, ROW, 2, pick_count), 0, 1 << 20) * pick_count + jnp.arange(pick_count)
    picked = jnp.take_along_axis(picked, jnp.argsort(mixing, axis=-1), axis=-1)
    parity = jnp.arange(2)[None, None, :, None]
    device_in_row = 2 * (picked // CAP) + parity
    row_start = (jnp.arange(groups_all) * ROW)[:, None, None, None]
    lower_view = jnp.arange(pick_count) % 2
    tile_number = 2 * (row_start + device_in_row) + lower_view
    tile_number = tile_number.reshape(groups_all, ROW, 2, BRICK_DEV, 2).transpose(0, 1, 3, 2, 4)
    return tile_number.reshape(BRICKS, 4).astype(jnp.int32)


def set_ends(drawn, stream_key, low, largest):
    longest = drawn.shape.index(max(drawn.shape))
    spots = []
    for shift in (0, 1):
        where = [jax.random.randint(jax.random.fold_in(stream_key, axis), (), 0, length) for axis, length in enumerate(drawn.shape)]
        where[longest] = (where[longest] + shift) % drawn.shape[longest]
        spots.append(tuple(where))
    return drawn.at[spots[0]].set(low).at[spots[1]].set(largest)


def level_of(own_key, dims, cuts, smallest, top_value):
    level, own = 1.0, jax.random.fold_in(own_key, 6)
    for dim, shards_of in cuts:
        heights = jnp.exp(jax.random.uniform(jax.random.fold_in(own, dim), (shards_of,), jnp.float32, smallest / len(cuts), top_value / len(cuts)))
        level = level * jnp.repeat(heights, dims[dim] // shards_of).reshape([-1 if axis == dim else 1 for axis in range(len(dims))])
    return level


def centred(key, shape, scale, bound, split=(), kind=jnp.bfloat16):
    result = scale * jax.random.normal(key, shape, jnp.float32)
    if split:
        result = result * level_of(key, shape, split, -0.22, 0.18)
    return jnp.clip(result, -bound, bound).astype(kind)


def setup_inputs(seed: int = 0) -> dict:
    seeds = jax.random.split(jax.random.key(seed), 10)
    return {
        "bricks": centred(seeds[0], (BRICKS, DEPTH, FOOT, FOOT), 1.0, 6.0, ((0, 32),)),
        "live": draw_live(jax.random.fold_in(seeds[9], 71), 0),
        "shear": jnp.clip(jax.random.uniform(seeds[2], (VIEWS, 2), jnp.float32, -1.0, 1.0), -1.0, 1.0),
        "offsets": set_ends(jax.random.randint(seeds[3], (BRICKS, VIEWS, 2), 0 - FOOT // 16, FOOT // 16 + 1), jax.random.fold_in(seeds[3], 1), 0 - FOOT // 16, (FOOT // 16 + 1) - 1).astype(jnp.int32),
        "absorb": jnp.clip(jnp.exp(math.log(0.119628906) - 1.7938024 * jax.random.uniform(seeds[4], (BRICKS,), jnp.float32) ** level_of(seeds[4], (BRICKS,), ((0, 32),), -0.2, 0.2)), 0.019897461, 0.119628906).astype(jnp.bfloat16),
        "color_gain": jnp.clip(jax.random.uniform(seeds[5], (3,), jnp.float32, 0.5, 3.0), 0.5, 3.0),
        "color_bias": jnp.clip(jax.random.uniform(seeds[6], (3,), jnp.float32, -1.0, 1.0), -1.0, 1.0),
        "targets": draw_targets(jax.random.fold_in(seeds[9], 71), 0),
        "order": jax.vmap(lambda own: jax.random.permutation(own, BRICKS))(jax.random.split(seeds[8], VIEWS)).reshape((VIEWS, BRICKS)).astype(jnp.int32),
    }


def interp_rows(shifted, extent):
    places = jnp.arange(extent, dtype=jnp.float32)
    spacing = places[:, None] - places[None, :] - shifted
    return jnp.maximum(0.0, 1.0 - jnp.abs(spacing)).astype(jnp.bfloat16)


def render(brick, live_count, absorb_rate, offset_pair, shear_pair, color_gain, color_bias):
    extent = brick.shape[-1]
    layers = brick.shape[0]
    offset_float = offset_pair.astype(jnp.float32)
    strength = absorb_rate.astype(jnp.float32)

    def advance(carry, inputs):
        colors, optical = carry
        layer, position = inputs
        raised = position.astype(jnp.float32) - jnp.float32(layers // 2)
        shifted = offset_float + raised * shear_pair
        across = interp_rows(shifted[0], extent)
        downward = interp_rows(shifted[1], extent)
        halfway = jnp.dot(across.astype(jnp.float32), layer.astype(jnp.float32), preferred_element_type=jnp.float32).astype(jnp.bfloat16)
        density = jnp.dot(halfway.astype(jnp.float32), downward.astype(jnp.float32).T, preferred_element_type=jnp.float32)
        thickness = jnp.where(position < live_count, strength * jax.nn.softplus(density), jnp.zeros_like(density))
        emitted = (1.0 - jnp.exp(-thickness))[None] * jax.nn.sigmoid(color_gain[:, None, None] * density[None] + color_bias[:, None, None])
        return (colors + jnp.exp(-optical)[None] * emitted, optical + thickness), None

    start = (jnp.zeros((3, extent, extent), jnp.float32), jnp.zeros((extent, extent), jnp.float32))
    (colors, optical), _ = lax.scan(advance, start, (brick, jnp.arange(layers, dtype=jnp.int32)))
    return colors.astype(jnp.bfloat16), optical.astype(jnp.bfloat16)


def reference(bricks, live, shear, offsets, absorb, color_gain, color_bias, targets, order):
    extent = bricks.shape[-1]
    color_image = jnp.zeros((TILES, 3, extent, extent), jnp.float32)
    depth_image = jnp.zeros((TILES, extent, extent), jnp.float32)
    for view in range(VIEWS):
        def visit(state, which):
            color_now, depth_now = state
            colors, optical = render(bricks[which], live[which], absorb[which], offsets[which, view], shear[view], color_gain, color_bias)
            target = targets[which, view].astype(jnp.int32)
            color_prior = lax.dynamic_index_in_dim(color_now, target, 0, keepdims=False)
            depth_prior = lax.dynamic_index_in_dim(depth_now, target, 0, keepdims=False)
            color_after = color_prior + jnp.exp(-depth_prior)[None] * colors.astype(jnp.float32)
            depth_after = depth_prior + optical.astype(jnp.float32)
            color_now = lax.dynamic_update_index_in_dim(color_now, color_after, target, 0)
            depth_now = lax.dynamic_update_index_in_dim(depth_now, depth_after, target, 0)
            return (color_now, depth_now), None

        sequence = jnp.argsort(order[view]).astype(jnp.int32)
        (color_image, depth_image), _ = lax.scan(visit, (color_image, depth_image), sequence)
    return jnp.concatenate([color_image, jnp.exp(-depth_image)[:, None]], axis=1)
```

```python
import functools

import jax
import jax.numpy as jnp
from jax import lax
from jax.experimental import pallas as pl
from jax.experimental.pallas import tpu as pltpu
from jax.sharding import PartitionSpec as P

MESH = pl.DeviceIdType.MESH
F32 = jnp.float32
BF16 = jnp.bfloat16
LANES = 128
ABSORB_UNIT = float(2**20)
OFF_X, OFF_Y, LIVE, VIEW, ABSORB, TILE, RANK, BRICK = range(8)


def table_kernel(row, capacity, targets, offsets, live, absorb, order, table, counts):
    bricks, views = targets.shape

    def clear(d, _):
        counts[d] = 0
        for c in range(capacity):
            for field in range(8):
                table[d, c, field] = -1 if field == TILE else 0
        return 0

    lax.fori_loop(0, row, clear, 0)

    def place(b, _):
        for v in range(views):
            tile = targets[b, v]
            d = lax.rem(lax.div(tile, 2), row)
            c = counts[d]
            counts[d] = c + 1
            table[d, c, OFF_X] = offsets[b, 2 * v]
            table[d, c, OFF_Y] = offsets[b, 2 * v + 1]
            table[d, c, LIVE] = live[b]
            table[d, c, VIEW] = v
            table[d, c, ABSORB] = absorb[b]
            table[d, c, TILE] = lax.rem(tile, 2)
            table[d, c, RANK] = order[v, b]
            table[d, c, BRICK] = b
        return 0

    lax.fori_loop(0, bricks, place, 0)


def main_kernel(
    ny, nz, capacity,
    table_s, table_v, bricks, shear, gain, bias,
    out,
    send_buf, recv_buf, recv_table, recv_scalar, sort_v, sort_s, spacing, foot, keys,
    table_send, table_recv, brick_send, brick_recv, local_sem,
):
    row = ny * nz
    slots = row * capacity
    layers, extent = bricks.shape[1], bricks.shape[2]
    my_y, my_z = lax.axis_index("gy"), lax.axis_index("gz")
    steps = [(0, 0)] + [
        (dy, dz)
        for dz in sorted(range(nz), key=lambda dz: -min(dz, nz - dz))
        for dy in range(ny)
        if (dy, dz) != (0, 0)
    ]

    def peer(e):
        dy, dz = steps[e]
        return lax.rem(my_y + dy, ny), lax.rem(my_z + dz, nz)

    barrier = pltpu.get_barrier_semaphore()
    for e in range(1, row):
        py, pz = peer(e)
        pl.semaphore_signal(barrier, inc=1, device_id={"gy": py, "gz": pz}, device_id_type=MESH)

    def table_copy(e, py, pz):
        return pltpu.make_async_remote_copy(
            src_ref=table_v.at[py * nz + pz], dst_ref=recv_table.at[e],
            send_sem=table_send.at[e], recv_sem=table_recv.at[e],
            device_id={"gy": py, "gz": pz}, device_id_type=MESH,
        )

    def brick_copy(e, py, pz):
        return pltpu.make_async_remote_copy(
            src_ref=send_buf.at[e], dst_ref=recv_buf.at[e],
            send_sem=brick_send.at[e], recv_sem=brick_recv.at[e],
            device_id={"gy": py, "gz": pz}, device_id_type=MESH,
        )

    def gather(e, py, pz, into):
        for c in range(capacity):
            into[e, c] = bricks[table_s[py * nz + pz, c, BRICK]]

    gather(1, *peer(1), send_buf)
    pl.semaphore_wait(barrier, row - 1)
    for e in range(1, row):
        table_copy(e, *peer(e)).start()
    for e in range(1, row):
        py, pz = peer(e)
        if e > 1:
            gather(e, py, pz, send_buf)
        brick_copy(e, py, pz).start()

    gather(0, my_y, my_z, recv_buf)
    recv_table[0] = table_v[my_y * nz + my_z]
    rows = lax.broadcasted_iota(jnp.int32, (extent, extent), 0)
    cols = lax.broadcasted_iota(jnp.int32, (extent, extent), 1)
    spacing[...] = (rows - cols).astype(F32)

    def table_arrived(e, _):
        table_copy(e, my_y, my_z).wait_recv()
        return 0

    lax.fori_loop(1, row, table_arrived, 0)
    to_scalar = pltpu.make_async_copy(recv_table, recv_scalar, local_sem.at[0])
    to_scalar.start()

    keys[...] = jnp.full(keys.shape, -1, jnp.int32)
    for e in range(row):
        keys[e * capacity:(e + 1) * capacity, :] = recv_table[e, 0:capacity, :]
    tile = keys[:, TILE:TILE + 1]
    key = jnp.where(tile < 0, 2, tile) * (1 << 20) + keys[:, RANK:RANK + 1]
    size = keys.shape[0]
    key = jnp.broadcast_to(key, (size, size))
    other = key.T
    me = lax.broadcasted_iota(jnp.int32, (size, size), 0)
    it = lax.broadcasted_iota(jnp.int32, (size, size), 1)
    ahead = (other < key) | ((other == key) & (it < me))
    place = jnp.sum(jnp.where(ahead, 1, 0), axis=1, keepdims=True)
    hit = place == it
    sort_v[0:1, :] = jnp.sum(jnp.where(hit, me, 0), axis=0, keepdims=True)
    sort_v[1:2, :] = jnp.sum(jnp.where(hit & (tile == 0), 1, 0), axis=0, keepdims=True)
    sort_v[2:3, :] = jnp.sum(jnp.where(hit & (tile == 1), 1, 0), axis=0, keepdims=True)
    to_sort = pltpu.make_async_copy(sort_v, sort_s, local_sem.at[1])
    to_sort.start()
    to_scalar.wait()
    to_sort.wait()

    def interp(shifted):
        return jnp.maximum(0.0, 1.0 - jnp.abs(spacing[...] - shifted)).astype(BF16)

    def render(e):
        for c in range(capacity):
            off_x = recv_scalar[e, c, OFF_X].astype(F32)
            off_y = recv_scalar[e, c, OFF_Y].astype(F32)
            count = recv_scalar[e, c, LIVE]
            view = recv_scalar[e, c, VIEW]
            strength = recv_scalar[e, c, ABSORB].astype(F32) * (1.0 / ABSORB_UNIT)
            optical, clear, colors = None, None, [None] * 3
            for k in range(layers):
                raised = float(k - layers // 2)
                across = interp(off_x + raised * shear[view, 0])
                downward = interp(off_y + raised * shear[view, 1])
                halfway = jnp.dot(across, recv_buf[e, c, k], preferred_element_type=F32).astype(BF16)
                density = lax.dot_general(
                    halfway, downward, (((1,), (1,)), ((), ())), preferred_element_type=F32
                )
                rate = jnp.where(k < count, strength, 0.0)
                soft = jnp.maximum(density, 0.0) + jnp.log(1.0 + jnp.exp(-jnp.abs(density)))
                thickness = rate * soft
                passed = jnp.exp(-thickness)
                half_alpha = 0.5 - 0.5 * passed
                if k:
                    half_alpha = half_alpha * clear
                for n in range(3):
                    lit = half_alpha + half_alpha * jnp.tanh(
                        (0.5 * gain[n]) * density + 0.5 * bias[n]
                    )
                    colors[n] = lit if k == 0 else colors[n] + lit
                optical = thickness if k == 0 else optical + thickness
                clear = passed if k == 0 else clear * passed
            for n in range(3):
                foot[e * capacity + c, n] = colors[n].astype(BF16)
            foot[e * capacity + c, 3] = optical.astype(BF16)

    render(0)

    def arrived(e, _):
        brick_copy(e, my_y, my_z).wait_recv()
        render(e)
        return 0

    lax.fori_loop(1, row, arrived, 0)

    def left(e, _):
        table_copy(e, my_y, my_z).wait_send()
        brick_copy(e, my_y, my_z).wait_send()
        return 0

    lax.fori_loop(1, row, left, 0)

    height = 16

    def strip(r, _):
        lines = pl.ds(pl.multiple_of(r * height, height), height)

        def visit(p, carry):
            optical0, optical1, color0, color1 = carry
            which = sort_s[0, p]
            in0 = sort_s[1, p].astype(F32)
            in1 = sort_s[2, p].astype(F32)
            clear = jnp.exp(-(optical0 * in0 + optical1 * in1))
            clear0, clear1 = clear * in0, clear * in1
            shade = [foot[which, n, lines, :].astype(F32) for n in range(3)]
            depth = foot[which, 3, lines, :].astype(F32)
            return (
                optical0 + in0 * depth,
                optical1 + in1 * depth,
                tuple(c + clear0 * s for c, s in zip(color0, shade)),
                tuple(c + clear1 * s for c, s in zip(color1, shade)),
            )

        zero = jnp.zeros((height, extent), F32)
        optical0, optical1, color0, color1 = lax.fori_loop(
            0, slots, visit, (zero, zero, (zero,) * 3, (zero,) * 3), unroll=4
        )
        for n in range(3):
            out[0, n, lines, :] = color0[n]
            out[1, n, lines, :] = color1[n]
        out[0, 3, lines, :] = jnp.exp(-optical0)
        out[1, 3, lines, :] = jnp.exp(-optical1)
        return 0

    lax.fori_loop(0, extent // height, strip, 0)


def body(ny, nz, bricks, live, shear, offsets, absorb, color_gain, color_bias, targets, order):
    brick_count, layers, extent, _ = bricks.shape
    views = shear.shape[0]
    row = ny * nz
    capacity = (brick_count * views + row - 1) // row
    slots = row * capacity
    smem = pl.BlockSpec(memory_space=pltpu.SMEM)
    vmem = pl.BlockSpec(memory_space=pltpu.VMEM)
    table_rows = (capacity + 7) // 8 * 8
    sort_size = (slots + LANES - 1) // LANES * LANES
    absorb_units = jnp.round(absorb.astype(F32) * ABSORB_UNIT).astype(jnp.int32)
    table = pl.pallas_call(
        functools.partial(table_kernel, row, capacity),
        out_shape=jax.ShapeDtypeStruct((row, table_rows, LANES), jnp.int32),
        in_specs=[smem] * 5,
        out_specs=smem,
        scratch_shapes=[pltpu.SMEM((row,), jnp.int32)],
    )(targets, offsets.reshape(brick_count, views * 2), live, absorb_units, order)
    return pl.pallas_call(
        functools.partial(main_kernel, ny, nz, capacity),
        out_shape=jax.ShapeDtypeStruct((2, 4, extent, extent), F32),
        in_specs=[smem, vmem, vmem, smem, smem, smem],
        out_specs=vmem,
        scratch_shapes=[
            pltpu.VMEM((row, capacity, layers, extent, extent), BF16),
            pltpu.VMEM((row, capacity, layers, extent, extent), BF16),
            pltpu.VMEM((row, table_rows, LANES), jnp.int32),
            pltpu.SMEM((row, table_rows, LANES), jnp.int32),
            pltpu.VMEM((8, sort_size), jnp.int32),
            pltpu.SMEM((8, sort_size), jnp.int32),
            pltpu.VMEM((extent, extent), F32),
            pltpu.VMEM((slots, 4, extent, extent), BF16),
            pltpu.VMEM((sort_size, LANES), jnp.int32),
            pltpu.SemaphoreType.DMA((row,)),
            pltpu.SemaphoreType.DMA((row,)),
            pltpu.SemaphoreType.DMA((row,)),
            pltpu.SemaphoreType.DMA((row,)),
            pltpu.SemaphoreType.DMA((2,)),
        ],
        compiler_params=pltpu.CompilerParams(
            collective_id=0, has_side_effects=True, vmem_limit_bytes=48 * 1024 * 1024
        ),
    )(table, table, bricks, shear, color_gain, color_bias)


def solution(mesh):
    ny, nz = mesh.shape["gy"], mesh.shape["gz"]
    split = ("gx", "gy", "gz")
    placed = (
        P(split, None, None, None),
        P(split),
        P(),
        P(split, None, None),
        P(split),
        P(),
        P(),
        P(split, None),
        P(None, split),
    )
    return jax.shard_map(
        functools.partial(body, ny, nz),
        mesh=mesh,
        in_specs=placed,
        out_specs=P(split, None, None, None),
        check_vma=False,
    )
```

```python
import functools

import jax
import jax.numpy as jnp
from jax import lax
from jax.experimental import pallas as pl
from jax.experimental.pallas import tpu as pltpu
from jax.sharding import PartitionSpec as P

MESH = pl.DeviceIdType.MESH
F32 = jnp.float32
BF16 = jnp.bfloat16
LANES = 128
ABSORB_UNIT = float(2**20)
OFF_X, OFF_Y, LIVE, VIEW, ABSORB, TILE, RANK, BRICK = range(8)


def main_kernel(
    ny, nz, capacity,
    bricks_in, live, shear, offsets, absorb, gain, bias, targets, order,
    out,
    bricks, send_buf, recv_buf, send_table, recv_table, raw, items, chosen_v, chosen_s,
    shift_v, shift_s, sort_v, sort_s, spacing, foot, keys,
    table_send, table_recv, brick_send, brick_recv, local_sem,
):
    row = ny * nz
    slots = row * capacity
    count, layers, extent, _ = bricks.shape
    views = targets.shape[1]
    size = keys.shape[0]
    my_y, my_z = lax.axis_index("gy"), lax.axis_index("gz")
    steps = [(0, 0)] + [
        (dy, dz)
        for dz in sorted(range(nz), key=lambda dz: -min(dz, nz - dz))
        for dy in range(ny)
        if (dy, dz) != (0, 0)
    ]

    def peer(e):
        dy, dz = steps[e]
        return lax.rem(my_y + dy, ny), lax.rem(my_z + dz, nz)

    barrier = pltpu.get_barrier_semaphore()
    for e in range(1, row):
        py, pz = peer(e)
        pl.semaphore_signal(barrier, inc=1, device_id={"gy": py, "gz": pz}, device_id_type=MESH)

    load_bricks = pltpu.make_async_copy(bricks_in, bricks, local_sem.at[0])
    load_bricks.start()

    raw[...] = jnp.zeros(raw.shape, jnp.int32)
    raw[0:views, 0:count] = order[...]
    raw[views:views + 1, 0:count] = live[...]
    units = jnp.round(absorb[...].astype(F32) * ABSORB_UNIT)
    raw[views + 1:views + 2, 0:count] = units.astype(jnp.int32)
    turned = raw[...].T
    items[...] = jnp.zeros(items.shape, jnp.int32)
    for v in range(views):
        mine = slice(v * count, (v + 1) * count)
        items[mine, OFF_X:OFF_Y + 1] = offsets[:, v, :]
        items[mine, LIVE:LIVE + 1] = turned[0:count, views:views + 1]
        items[mine, VIEW:VIEW + 1] = jnp.full((count, 1), v, jnp.int32)
        items[mine, ABSORB:ABSORB + 1] = turned[0:count, views + 1:views + 2]
        items[mine, TILE:TILE + 1] = targets[:, v:v + 1]
        items[mine, RANK:RANK + 1] = turned[0:count, v:v + 1]
        items[mine, BRICK:BRICK + 1] = lax.broadcasted_iota(jnp.int32, (count, 1), 0)
    me = lax.broadcasted_iota(jnp.int32, (size, size), 0)
    it = lax.broadcasted_iota(jnp.int32, (size, size), 1)
    used = views * count
    owner = jnp.where(me < used, lax.rem(lax.div(items[:, TILE:TILE + 1], 2), row), -1)
    same = (owner == owner.T) & (it < me)
    slot = owner * capacity + jnp.sum(jnp.where(same, 1, 0), axis=1, keepdims=True)
    slot = jnp.where(me < used, slot, -1)
    chosen_v[0:1, :] = jnp.sum(
        jnp.where(slot == it, items[:, BRICK:BRICK + 1], 0), axis=0, keepdims=True
    )
    load_chosen = pltpu.make_async_copy(chosen_v, chosen_s, local_sem.at[1])
    load_chosen.start()
    hit = (slot.T == me)[0:slots, :]
    lane = lax.broadcasted_iota(jnp.int32, (slots, LANES), 1)
    table = jnp.where(lane == TILE, -1, 0)
    entry = jnp.where(lane[0:1, :] == TILE, lax.rem(items[...], 2) + 1, items[...])
    hit_int = jnp.where(hit, 1, 0)
    for i in range(used):
        table = table + hit_int[:, i:i + 1] * entry[i:i + 1, :]
    for d in range(row):
        send_table[d, 0:capacity, :] = table[d * capacity:(d + 1) * capacity, :]

    def table_copy(e, py, pz):
        return pltpu.make_async_remote_copy(
            src_ref=send_table.at[py * nz + pz], dst_ref=recv_table.at[e],
            send_sem=table_send.at[e], recv_sem=table_recv.at[e],
            device_id={"gy": py, "gz": pz}, device_id_type=MESH,
        )

    def brick_copy(e, py, pz):
        return pltpu.make_async_remote_copy(
            src_ref=send_buf.at[e], dst_ref=recv_buf.at[e],
            send_sem=brick_send.at[e], recv_sem=brick_recv.at[e],
            device_id={"gy": py, "gz": pz}, device_id_type=MESH,
        )

    def gather(e, py, pz, into):
        for c in range(capacity):
            into[e, c] = bricks[chosen_s[0, (py * nz + pz) * capacity + c]]

    load_bricks.wait()
    load_chosen.wait()
    gather(1, *peer(1), send_buf)
    pl.semaphore_wait(barrier, row - 1)
    for e in range(1, row):
        table_copy(e, *peer(e)).start()
    for e in range(1, row):
        py, pz = peer(e)
        if e > 1:
            gather(e, py, pz, send_buf)
        brick_copy(e, py, pz).start()

    gather(0, my_y, my_z, recv_buf)
    recv_table[0] = send_table[my_y * nz + my_z]
    rows = lax.broadcasted_iota(jnp.int32, (extent, extent), 0)
    cols = lax.broadcasted_iota(jnp.int32, (extent, extent), 1)
    spacing[...] = (rows - cols).astype(F32)

    def table_arrived(e, _):
        table_copy(e, my_y, my_z).wait_recv()
        return 0

    lax.fori_loop(1, row, table_arrived, 0)
    keys[...] = jnp.full(keys.shape, -1, jnp.int32)
    for e in range(row):
        keys[e * capacity:(e + 1) * capacity, :] = recv_table[e, 0:capacity, :]
    view = keys[:, VIEW:VIEW + 1]
    for axis in range(2):
        slope = jnp.zeros((size, 1), F32)
        for v in range(views):
            slope = jnp.where(view == v, shear[v:v + 1, axis:axis + 1], slope)
        offset = keys[:, OFF_X + axis:OFF_X + axis + 1].astype(F32)
        for k in range(layers):
            shift_v[:, 3 * k + axis:3 * k + axis + 1] = offset + float(k - layers // 2) * slope
    strength = keys[:, ABSORB:ABSORB + 1].astype(F32) * (1.0 / ABSORB_UNIT)
    for k in range(layers):
        shift_v[:, 3 * k + 2:3 * k + 3] = jnp.where(keys[:, LIVE:LIVE + 1] > k, strength, 0.0)
    to_shift = pltpu.make_async_copy(shift_v, shift_s, local_sem.at[3])
    to_shift.start()
    tile = keys[:, TILE:TILE + 1]
    key = jnp.where(tile < 0, 2, tile) * (1 << 20) + keys[:, RANK:RANK + 1]
    key = jnp.broadcast_to(key, (size, size))
    other = key.T
    ahead = (other < key) | ((other == key) & (it < me))
    place = jnp.sum(jnp.where(ahead, 1, 0), axis=1, keepdims=True)
    hit = place == it
    sort_v[0:1, :] = jnp.sum(jnp.where(hit, me, 0), axis=0, keepdims=True)
    sort_v[1:2, :] = jnp.sum(jnp.where(hit & (tile == 0), 1, 0), axis=0, keepdims=True)
    sort_v[2:3, :] = jnp.sum(jnp.where(hit & (tile == 1), 1, 0), axis=0, keepdims=True)
    to_sort = pltpu.make_async_copy(sort_v, sort_s, local_sem.at[2])
    to_sort.start()
    to_shift.wait()
    to_sort.wait()

    def interp(shifted):
        return jnp.maximum(0.0, 1.0 - jnp.abs(spacing[...] - shifted)).astype(BF16)

    def render(e):
        for c in range(capacity):
            spot = e * capacity + c
            optical, clear, colors = None, None, [None] * 3
            for k in range(layers):
                across = interp(shift_s[spot, 3 * k])
                downward = interp(shift_s[spot, 3 * k + 1])
                halfway = jnp.dot(across, recv_buf[e, c, k], preferred_element_type=F32).astype(BF16)
                density = lax.dot_general(
                    halfway, downward, (((1,), (1,)), ((), ())), preferred_element_type=F32
                )
                rate = shift_s[spot, 3 * k + 2]
                soft = jnp.maximum(density, 0.0) + jnp.log(1.0 + jnp.exp(-jnp.abs(density)))
                thickness = rate * soft
                passed = jnp.exp(-thickness)
                half_alpha = 0.5 - 0.5 * passed
                if k:
                    half_alpha = half_alpha * clear
                for n in range(3):
                    lit = half_alpha + half_alpha * jnp.tanh(
                        (0.5 * gain[n]) * density + 0.5 * bias[n]
                    )
                    colors[n] = lit if k == 0 else colors[n] + lit
                optical = thickness if k == 0 else optical + thickness
                clear = passed if k == 0 else clear * passed
            for n in range(3):
                foot[spot, n] = colors[n].astype(BF16)
            foot[spot, 3] = optical.astype(BF16)

    render(0)

    def arrived(e, _):
        brick_copy(e, my_y, my_z).wait_recv()
        render(e)
        return 0

    lax.fori_loop(1, row, arrived, 0)

    def left(e, _):
        table_copy(e, my_y, my_z).wait_send()
        brick_copy(e, my_y, my_z).wait_send()
        return 0

    lax.fori_loop(1, row, left, 0)

    height = 16

    def strip(r, _):
        lines = pl.ds(pl.multiple_of(r * height, height), height)

        def visit(p, carry):
            optical0, optical1, color0, color1 = carry
            which = sort_s[0, p]
            in0 = sort_s[1, p].astype(F32)
            in1 = sort_s[2, p].astype(F32)
            clear = jnp.exp(-(optical0 * in0 + optical1 * in1))
            clear0, clear1 = clear * in0, clear * in1
            shade = [foot[which, n, lines, :].astype(F32) for n in range(3)]
            depth = foot[which, 3, lines, :].astype(F32)
            return (
                optical0 + in0 * depth,
                optical1 + in1 * depth,
                tuple(c + clear0 * s for c, s in zip(color0, shade)),
                tuple(c + clear1 * s for c, s in zip(color1, shade)),
            )

        zero = jnp.zeros((height, extent), F32)
        optical0, optical1, color0, color1 = lax.fori_loop(
            0, slots, visit, (zero, zero, (zero,) * 3, (zero,) * 3), unroll=4
        )
        for n in range(3):
            out[0, n, lines, :] = color0[n]
            out[1, n, lines, :] = color1[n]
        out[0, 3, lines, :] = jnp.exp(-optical0)
        out[1, 3, lines, :] = jnp.exp(-optical1)
        return 0

    lax.fori_loop(0, extent // height, strip, 0)


def body(ny, nz, bricks, live, shear, offsets, absorb, color_gain, color_bias, targets, order):
    brick_count, layers, extent, _ = bricks.shape
    views = shear.shape[0]
    row = ny * nz
    capacity = (brick_count * views + row - 1) // row
    slots = row * capacity
    smem = pl.BlockSpec(memory_space=pltpu.SMEM)
    vmem = pl.BlockSpec(memory_space=pltpu.VMEM)
    table_rows = (capacity + 7) // 8 * 8
    longest = max(slots, brick_count * views)
    size = (longest + LANES - 1) // LANES * LANES
    return pl.pallas_call(
        functools.partial(main_kernel, ny, nz, capacity),
        out_shape=jax.ShapeDtypeStruct((2, 4, extent, extent), F32),
        in_specs=[pl.BlockSpec(memory_space=pl.ANY), vmem, vmem, vmem, vmem, smem, smem, vmem, vmem],
        out_specs=vmem,
        scratch_shapes=[
            pltpu.VMEM(bricks.shape, BF16),
            pltpu.VMEM((row, capacity, layers, extent, extent), BF16),
            pltpu.VMEM((row, capacity, layers, extent, extent), BF16),
            pltpu.VMEM((row, table_rows, LANES), jnp.int32),
            pltpu.VMEM((row, table_rows, LANES), jnp.int32),
            pltpu.VMEM((LANES, LANES), jnp.int32),
            pltpu.VMEM((size, LANES), jnp.int32),
            pltpu.VMEM((8, size), jnp.int32),
            pltpu.SMEM((8, size), jnp.int32),
            pltpu.VMEM((size, LANES), F32),
            pltpu.SMEM((size, LANES), F32),
            pltpu.VMEM((8, size), jnp.int32),
            pltpu.SMEM((8, size), jnp.int32),
            pltpu.VMEM((extent, extent), F32),
            pltpu.VMEM((slots, 4, extent, extent), BF16),
            pltpu.VMEM((size, LANES), jnp.int32),
            pltpu.SemaphoreType.DMA((row,)),
            pltpu.SemaphoreType.DMA((row,)),
            pltpu.SemaphoreType.DMA((row,)),
            pltpu.SemaphoreType.DMA((row,)),
            pltpu.SemaphoreType.DMA((4,)),
        ],
        compiler_params=pltpu.CompilerParams(
            collective_id=0, has_side_effects=True, vmem_limit_bytes=48 * 1024 * 1024
        ),
    )(
        bricks, live.reshape(1, brick_count), shear, offsets, absorb.reshape(1, brick_count),
        color_gain, color_bias, targets, order,
    )


def solution(mesh):
    ny, nz = mesh.shape["gy"], mesh.shape["gz"]
    split = ("gx", "gy", "gz")
    placed = (
        P(split, None, None, None),
        P(split),
        P(),
        P(split, None, None),
        P(split),
        P(),
        P(),
        P(split, None),
        P(None, split),
    )
    return jax.shard_map(
        functools.partial(body, ny, nz),
        mesh=mesh,
        in_specs=placed,
        out_specs=P(split, None, None, None),
        check_vma=False,
    )
```

```python
import functools

import jax
import jax.numpy as jnp
from jax import lax
from jax.experimental import pallas as pl
from jax.experimental.pallas import tpu as pltpu
from jax.sharding import PartitionSpec as P

MESH = pl.DeviceIdType.MESH
F32 = jnp.float32
BF16 = jnp.bfloat16
LANES = 128
ABSORB_UNIT = float(2**20)
OFF_X, OFF_Y, LIVE, VIEW, ABSORB, TILE, RANK, BRICK = range(8)


def main_kernel(
    ny, nz, capacity,
    bricks_in, live, shear, offsets, absorb, gain, bias, targets, order,
    out,
    bricks, raw_buf, relay_buf, raw_chosen_v, raw_chosen_s, send_buf, recv_buf, send_table, recv_table, raw, items, chosen_v, chosen_s,
    shift_v, shift_s, sort_v, sort_s, spacing, foot, keys,
    table_send, table_recv, brick_send, brick_recv, raw_send, raw_recv, forward_send, relay_send,
    local_sem,
):
    row = ny * nz
    slots = row * capacity
    count, layers, extent, _ = bricks.shape
    views = targets.shape[1]
    size = keys.shape[0]
    my_y, my_z = lax.axis_index("gy"), lax.axis_index("gz")
    half = nz // 2
    relayed = nz >= 4
    upper = my_z >= half
    inner = (my_z == half) | (my_z == half - 1)
    holder = inner | (my_z == half + 1) | (my_z == half - 2)

    def mirror(dz):
        return jnp.where(upper, dz, lax.rem(nz - dz, nz))

    def leaves_raw(dz):
        skip = mirror(dz)
        return inner & ((skip == nz - 1) | (skip == nz - 2)) if relayed else False

    def come(t):
        if t == 0:
            return jnp.int32(0)
        first = {1: nz - 1, 2: 1}.get(t, t - 1)
        return mirror(jnp.where(inner, first, t) if relayed else jnp.int32(t))

    def go(t):
        return mirror(jnp.where(inner, t, nz - t) if relayed else jnp.int32(t))

    def peer(dy, dz):
        return lax.rem(my_y + dy, ny), lax.rem(my_z + dz, nz)

    barrier = pltpu.get_barrier_semaphore()
    for e in range(1, row):
        py, pz = peer(e % ny, e // ny)
        pl.semaphore_signal(barrier, inc=1, device_id={"gy": py, "gz": pz}, device_id_type=MESH)

    load_bricks = pltpu.make_async_copy(bricks_in, bricks, local_sem.at[0])
    load_bricks.start()

    raw[...] = jnp.zeros(raw.shape, jnp.int32)
    raw[0:views, 0:count] = order[...]
    raw[views:views + 1, 0:count] = live[...]
    units = jnp.round(absorb[...].astype(F32) * ABSORB_UNIT)
    raw[views + 1:views + 2, 0:count] = units.astype(jnp.int32)
    turned = raw[...].T
    items[...] = jnp.zeros(items.shape, jnp.int32)
    for v in range(views):
        mine = slice(v * count, (v + 1) * count)
        items[mine, OFF_X:OFF_Y + 1] = offsets[:, v, :]
        items[mine, LIVE:LIVE + 1] = turned[0:count, views:views + 1]
        items[mine, VIEW:VIEW + 1] = jnp.full((count, 1), v, jnp.int32)
        items[mine, ABSORB:ABSORB + 1] = turned[0:count, views + 1:views + 2]
        items[mine, TILE:TILE + 1] = targets[:, v:v + 1]
        items[mine, RANK:RANK + 1] = turned[0:count, v:v + 1]
        items[mine, BRICK:BRICK + 1] = lax.broadcasted_iota(jnp.int32, (count, 1), 0)
    me = lax.broadcasted_iota(jnp.int32, (size, size), 0)
    it = lax.broadcasted_iota(jnp.int32, (size, size), 1)
    used = views * count
    owner = jnp.where(me < used, lax.rem(lax.div(items[:, TILE:TILE + 1], 2), row), -1)
    same = (owner == owner.T) & (it < me)
    slot = owner * capacity + jnp.sum(jnp.where(same, 1, 0), axis=1, keepdims=True)
    slot = jnp.where(me < used, slot, -1)
    chosen_v[0:1, :] = jnp.sum(
        jnp.where(slot == it, items[:, BRICK:BRICK + 1], 0), axis=0, keepdims=True
    )
    load_chosen = pltpu.make_async_copy(chosen_v, chosen_s, local_sem.at[1])
    load_chosen.start()
    hit = (slot.T == me)[0:slots, :]
    lane = lax.broadcasted_iota(jnp.int32, (slots, LANES), 1)
    table = jnp.where(lane == TILE, -1, 0)
    entry = jnp.where(lane[0:1, :] == TILE, lax.rem(items[...], 2) + 1, items[...])
    hit_int = jnp.where(hit, 1, 0)
    for i in range(used):
        table = table + hit_int[:, i:i + 1] * entry[i:i + 1, :]
    for d in range(row):
        send_table[d, 0:capacity, :] = table[d * capacity:(d + 1) * capacity, :]

    def table_copy(e, py, pz):
        return pltpu.make_async_remote_copy(
            src_ref=send_table.at[py * nz + pz], dst_ref=recv_table.at[e],
            send_sem=table_send.at[e], recv_sem=table_recv.at[e],
            device_id={"gy": py, "gz": pz}, device_id_type=MESH,
        )

    def brick_copy(e, py, pz):
        return pltpu.make_async_remote_copy(
            src_ref=send_buf.at[e], dst_ref=recv_buf.at[e],
            send_sem=brick_send.at[e], recv_sem=brick_recv.at[e],
            device_id={"gy": py, "gz": pz}, device_id_type=MESH,
        )

    def relay_copy(dy, dz, py, pz):
        return pltpu.make_async_remote_copy(
            src_ref=relay_buf.at[dy], dst_ref=recv_buf.at[dz * ny + dy],
            send_sem=relay_send.at[dy], recv_sem=brick_recv.at[dz * ny + dy],
            device_id={"gy": py, "gz": pz}, device_id_type=MESH,
        )

    def gather(source, chosen, py, pz, into, e):
        for c in range(capacity):
            into[e, c] = source[chosen[0, (py * nz + pz) * capacity + c]]

    def send(dy, dz):
        def direct():
            e = dz * ny + dy
            py, pz = peer(dy, dz)
            gather(bricks, chosen_s, py, pz, send_buf, e)
            brick_copy(e, py, pz).start()

        if relayed:
            pl.when(jnp.logical_not(leaves_raw(dz)))(direct)
        else:
            direct()

    pieces = ny if count % ny == 0 else 1
    depth = count // pieces
    partner = 2 * half - 1 - my_z
    beyond = jnp.where(upper, half + 1, half - 2)

    def raw_copy(j, source, sent, pz):
        part = pl.ds(j * depth, depth)
        return pltpu.make_async_remote_copy(
            src_ref=source.at[part], dst_ref=raw_buf.at[part],
            send_sem=sent.at[j], recv_sem=raw_recv.at[j],
            device_id={"gy": my_y, "gz": pz}, device_id_type=MESH,
        )

    def raw_chosen_copy(source, sent, pz):
        return pltpu.make_async_remote_copy(
            src_ref=source, dst_ref=raw_chosen_v,
            send_sem=sent.at[pieces], recv_sem=raw_recv.at[pieces],
            device_id={"gy": my_y, "gz": pz}, device_id_type=MESH,
        )

    load_bricks.wait()
    load_chosen.wait()
    pl.semaphore_wait(barrier, row - 1)
    if relayed:
        @pl.when(inner)
        def _():
            raw_copy(0, bricks, raw_send, partner).start()
            raw_chosen_copy(chosen_v, raw_send, partner).start()

    for e in range(1, row):
        table_copy(e, *peer(e % ny, e // ny)).start()
    for dy in range(ny):
        send(dy, go(1))
        if dy:
            send(dy, jnp.int32(0))
        if relayed and 0 < dy < pieces:
            @pl.when(inner)
            def _():
                raw_copy(dy, bricks, raw_send, partner).start()

    for t in range(2, nz):
        for dy in range(ny):
            send(dy, go(t))

    gather(bricks, chosen_s, my_y, my_z, recv_buf, 0)
    recv_table[0] = send_table[my_y * nz + my_z]
    rows = lax.broadcasted_iota(jnp.int32, (extent, extent), 0)
    cols = lax.broadcasted_iota(jnp.int32, (extent, extent), 1)
    spacing[...] = (rows - cols).astype(F32)

    def table_arrived(e, _):
        table_copy(e, my_y, my_z).wait_recv()
        return 0

    lax.fori_loop(1, row, table_arrived, 0)
    keys[...] = jnp.full(keys.shape, -1, jnp.int32)
    for e in range(row):
        keys[e * capacity:(e + 1) * capacity, :] = recv_table[e, 0:capacity, :]
    view = keys[:, VIEW:VIEW + 1]
    for axis in range(2):
        slope = jnp.zeros((size, 1), F32)
        for v in range(views):
            slope = jnp.where(view == v, shear[v:v + 1, axis:axis + 1], slope)
        offset = keys[:, OFF_X + axis:OFF_X + axis + 1].astype(F32)
        for k in range(layers):
            shift_v[:, 3 * k + axis:3 * k + axis + 1] = offset + float(k - layers // 2) * slope
    strength = keys[:, ABSORB:ABSORB + 1].astype(F32) * (1.0 / ABSORB_UNIT)
    for k in range(layers):
        shift_v[:, 3 * k + 2:3 * k + 3] = jnp.where(keys[:, LIVE:LIVE + 1] > k, strength, 0.0)
    to_shift = pltpu.make_async_copy(shift_v, shift_s, local_sem.at[3])
    to_shift.start()
    tile = keys[:, TILE:TILE + 1]
    key = jnp.where(tile < 0, 2, tile) * (1 << 20) + keys[:, RANK:RANK + 1]
    key = jnp.broadcast_to(key, (size, size))
    other = key.T
    ahead = (other < key) | ((other == key) & (it < me))
    place = jnp.sum(jnp.where(ahead, 1, 0), axis=1, keepdims=True)
    hit = place == it
    sort_v[0:1, :] = jnp.sum(jnp.where(hit, me, 0), axis=0, keepdims=True)
    sort_v[1:2, :] = jnp.sum(jnp.where(hit & (tile == 0), 1, 0), axis=0, keepdims=True)
    sort_v[2:3, :] = jnp.sum(jnp.where(hit & (tile == 1), 1, 0), axis=0, keepdims=True)
    to_sort = pltpu.make_async_copy(sort_v, sort_s, local_sem.at[2])
    to_sort.start()
    to_shift.wait()
    to_sort.wait()

    def interp(shifted):
        return jnp.maximum(0.0, 1.0 - jnp.abs(spacing[...] - shifted)).astype(BF16)

    def render(e):
        for c in range(capacity):
            spot = e * capacity + c
            optical, clear, colors = None, None, [None] * 3
            for k in range(layers):
                across = interp(shift_s[spot, 3 * k])
                downward = interp(shift_s[spot, 3 * k + 1])
                halfway = jnp.dot(across, recv_buf[e, c, k], preferred_element_type=F32).astype(BF16)
                density = lax.dot_general(
                    halfway, downward, (((1,), (1,)), ((), ())), preferred_element_type=F32
                )
                rate = shift_s[spot, 3 * k + 2]
                soft = jnp.maximum(density, 0.0) + jnp.log(1.0 + jnp.exp(-jnp.abs(density)))
                thickness = rate * soft
                passed = jnp.exp(-thickness)
                half_alpha = 0.5 - 0.5 * passed
                if k:
                    half_alpha = half_alpha * clear
                for n in range(3):
                    lit = half_alpha + half_alpha * jnp.tanh(
                        (0.5 * gain[n]) * density + 0.5 * bias[n]
                    )
                    colors[n] = lit if k == 0 else colors[n] + lit
                optical = thickness if k == 0 else optical + thickness
                clear = passed if k == 0 else clear * passed
            for n in range(3):
                foot[spot, n] = colors[n].astype(BF16)
            foot[spot, 3] = optical.astype(BF16)

    def arrived(e):
        brick_copy(e, my_y, my_z).wait_recv()

    def plain(first, dz):
        def step(dy, _):
            arrived(dz * ny + dy)
            render(dz * ny + dy)
            return 0

        lax.fori_loop(first, ny, step, 0)

    render(jnp.int32(0))
    plain(1, jnp.int32(0))
    for t in range(1, nz):
        dz = come(t)
        if relayed and t == 1:
            @pl.when(inner)
            def _():
                raw_chosen_copy(chosen_v, raw_send, partner).wait_recv()
                raw_chosen_copy(raw_chosen_v, forward_send, beyond).start()

            def step(dy, _):
                @pl.when(inner & (dy < pieces))
                def _():
                    raw_copy(dy, bricks, raw_send, partner).wait_recv()
                    raw_copy(dy, raw_buf, forward_send, beyond).start()

                arrived(dz * ny + dy)
                render(dz * ny + dy)
                return 0

            lax.fori_loop(0, ny, step, 0)
        elif relayed and t == 2:
            @pl.when(holder)
            def _():
                @pl.when(jnp.logical_not(inner))
                def _():
                    raw_chosen_copy(chosen_v, raw_send, partner).wait_recv()
                    for j in range(pieces):
                        raw_copy(j, bricks, raw_send, partner).wait_recv()

                load_raw_chosen = pltpu.make_async_copy(raw_chosen_v, raw_chosen_s, local_sem.at[4])
                load_raw_chosen.start()
                load_raw_chosen.wait()
                for dy in range(1, ny):
                    py, pz = peer(dy, 0)
                    gather(raw_buf, raw_chosen_s, py, pz, relay_buf, dy)
                    relay_copy(dy, dz, py, pz).start()
                gather(raw_buf, raw_chosen_s, my_y, my_z, recv_buf, dz * ny)

            @pl.when(jnp.logical_not(holder))
            def _():
                arrived(dz * ny)

            render(dz * ny)
            plain(1, dz)
        else:
            plain(0, dz)

    def left(e, _):
        table_copy(e, my_y, my_z).wait_send()

        def direct():
            brick_copy(e, my_y, my_z).wait_send()

        if relayed:
            pl.when(jnp.logical_not(leaves_raw(lax.div(e, ny))))(direct)
        else:
            direct()
        return 0

    lax.fori_loop(1, row, left, 0)
    if relayed:
        @pl.when(inner)
        def _():
            for j in range(pieces):
                raw_copy(j, bricks, raw_send, partner).wait_send()
                raw_copy(j, raw_buf, forward_send, beyond).wait_send()
            raw_chosen_copy(chosen_v, raw_send, partner).wait_send()
            raw_chosen_copy(raw_chosen_v, forward_send, beyond).wait_send()

        @pl.when(holder)
        def _():
            for dy in range(1, ny):
                relay_copy(dy, jnp.int32(0), my_y, my_z).wait_send()

    height = 16

    def strip(r, _):
        lines = pl.ds(pl.multiple_of(r * height, height), height)

        def visit(p, carry):
            optical0, optical1, color0, color1 = carry
            which = sort_s[0, p]
            in0 = sort_s[1, p].astype(F32)
            in1 = sort_s[2, p].astype(F32)
            clear = jnp.exp(-(optical0 * in0 + optical1 * in1))
            clear0, clear1 = clear * in0, clear * in1
            shade = [foot[which, n, lines, :].astype(F32) for n in range(3)]
            depth = foot[which, 3, lines, :].astype(F32)
            return (
                optical0 + in0 * depth,
                optical1 + in1 * depth,
                tuple(c + clear0 * s for c, s in zip(color0, shade)),
                tuple(c + clear1 * s for c, s in zip(color1, shade)),
            )

        zero = jnp.zeros((height, extent), F32)
        optical0, optical1, color0, color1 = lax.fori_loop(
            0, slots, visit, (zero, zero, (zero,) * 3, (zero,) * 3), unroll=4
        )
        for n in range(3):
            out[0, n, lines, :] = color0[n]
            out[1, n, lines, :] = color1[n]
        out[0, 3, lines, :] = jnp.exp(-optical0)
        out[1, 3, lines, :] = jnp.exp(-optical1)
        return 0

    lax.fori_loop(0, extent // height, strip, 0)


def body(ny, nz, bricks, live, shear, offsets, absorb, color_gain, color_bias, targets, order):
    brick_count, layers, extent, _ = bricks.shape
    views = shear.shape[0]
    row = ny * nz
    capacity = (brick_count * views + row - 1) // row
    slots = row * capacity
    smem = pl.BlockSpec(memory_space=pltpu.SMEM)
    vmem = pl.BlockSpec(memory_space=pltpu.VMEM)
    table_rows = (capacity + 7) // 8 * 8
    longest = max(slots, brick_count * views)
    size = (longest + LANES - 1) // LANES * LANES
    return pl.pallas_call(
        functools.partial(main_kernel, ny, nz, capacity),
        out_shape=jax.ShapeDtypeStruct((2, 4, extent, extent), F32),
        in_specs=[pl.BlockSpec(memory_space=pl.ANY), vmem, vmem, vmem, vmem, smem, smem, vmem, vmem],
        out_specs=vmem,
        scratch_shapes=[
            pltpu.VMEM(bricks.shape, BF16),
            pltpu.VMEM(bricks.shape, BF16),
            pltpu.VMEM((ny, capacity, layers, extent, extent), BF16),
            pltpu.VMEM((8, size), jnp.int32),
            pltpu.SMEM((8, size), jnp.int32),
            pltpu.VMEM((row, capacity, layers, extent, extent), BF16),
            pltpu.VMEM((row, capacity, layers, extent, extent), BF16),
            pltpu.VMEM((row, table_rows, LANES), jnp.int32),
            pltpu.VMEM((row, table_rows, LANES), jnp.int32),
            pltpu.VMEM((LANES, LANES), jnp.int32),
            pltpu.VMEM((size, LANES), jnp.int32),
            pltpu.VMEM((8, size), jnp.int32),
            pltpu.SMEM((8, size), jnp.int32),
            pltpu.VMEM((size, LANES), F32),
            pltpu.SMEM((size, LANES), F32),
            pltpu.VMEM((8, size), jnp.int32),
            pltpu.SMEM((8, size), jnp.int32),
            pltpu.VMEM((extent, extent), F32),
            pltpu.VMEM((slots, 4, extent, extent), BF16),
            pltpu.VMEM((size, LANES), jnp.int32),
            pltpu.SemaphoreType.DMA((row,)),
            pltpu.SemaphoreType.DMA((row,)),
            pltpu.SemaphoreType.DMA((row,)),
            pltpu.SemaphoreType.DMA((row,)),
            pltpu.SemaphoreType.DMA((ny + 1,)),
            pltpu.SemaphoreType.DMA((ny + 1,)),
            pltpu.SemaphoreType.DMA((ny + 1,)),
            pltpu.SemaphoreType.DMA((ny,)),
            pltpu.SemaphoreType.DMA((5,)),
        ],
        compiler_params=pltpu.CompilerParams(
            collective_id=0, has_side_effects=True, vmem_limit_bytes=48 * 1024 * 1024
        ),
    )(
        bricks, live.reshape(1, brick_count), shear, offsets, absorb.reshape(1, brick_count),
        color_gain, color_bias, targets, order,
    )


def solution(mesh):
    ny, nz = mesh.shape["gy"], mesh.shape["gz"]
    split = ("gx", "gy", "gz")
    placed = (
        P(split, None, None, None),
        P(split),
        P(),
        P(split, None, None),
        P(split),
        P(),
        P(),
        P(split, None),
        P(None, split),
    )
    return jax.shard_map(
        functools.partial(body, ny, nz),
        mesh=mesh,
        in_specs=placed,
        out_specs=P(split, None, None, None),
        check_vma=False,
    )
```

```python
import functools

import jax
import jax.numpy as jnp
from jax import lax
from jax.experimental import pallas as pl
from jax.experimental.pallas import tpu as pltpu
from jax.sharding import PartitionSpec as P

MESH = pl.DeviceIdType.MESH
F32 = jnp.float32
BF16 = jnp.bfloat16
LANES = 128
ABSORB_UNIT = float(2**20)
OFF_X, OFF_Y, LIVE, VIEW, ABSORB, TILE, RANK, BRICK = range(8)


def main_kernel(
    ny, nz, capacity,
    bricks_in, live, shear, offsets, absorb, gain, bias, targets, order,
    out,
    bricks, raw_buf, relay_buf, raw_chosen_v, raw_chosen_s, send_buf, recv_buf, send_table, recv_table, raw, items, chosen_v, chosen_s,
    shift_v, shift_s, sort_v, sort_s, spacing, dense, foot, keys,
    table_send, table_recv, brick_send, brick_recv, raw_send, raw_recv, forward_send, relay_send,
    local_sem,
):
    row = ny * nz
    slots = row * capacity
    count, layers, extent, _ = bricks.shape
    views = targets.shape[1]
    size = keys.shape[0]
    my_y, my_z = lax.axis_index("gy"), lax.axis_index("gz")
    half = nz // 2
    relayed = nz >= 4
    upper = my_z >= half
    inner = (my_z == half) | (my_z == half - 1)
    holder = inner | (my_z == half + 1) | (my_z == half - 2)

    def mirror(dz):
        return jnp.where(upper, dz, lax.rem(nz - dz, nz))

    def leaves_raw(dz):
        skip = mirror(dz)
        return inner & ((skip == nz - 1) | (skip == nz - 2)) if relayed else False

    def come(t):
        if t == 0:
            return jnp.int32(0)
        first = {1: nz - 1, 2: 1}.get(t, t - 1)
        return mirror(jnp.where(inner, first, t) if relayed else jnp.int32(t))

    def go(t):
        return mirror(jnp.where(inner, t, nz - t) if relayed else jnp.int32(t))

    def peer(dy, dz):
        return lax.rem(my_y + dy, ny), lax.rem(my_z + dz, nz)

    barrier = pltpu.get_barrier_semaphore()
    for e in range(1, row):
        py, pz = peer(e % ny, e // ny)
        pl.semaphore_signal(barrier, inc=1, device_id={"gy": py, "gz": pz}, device_id_type=MESH)

    load_bricks = pltpu.make_async_copy(bricks_in, bricks, local_sem.at[0])
    load_bricks.start()

    raw[...] = jnp.zeros(raw.shape, jnp.int32)
    raw[0:views, 0:count] = order[...]
    raw[views:views + 1, 0:count] = live[...]
    units = jnp.round(absorb[...].astype(F32) * ABSORB_UNIT)
    raw[views + 1:views + 2, 0:count] = units.astype(jnp.int32)
    turned = raw[...].T
    items[...] = jnp.zeros(items.shape, jnp.int32)
    for v in range(views):
        mine = slice(v * count, (v + 1) * count)
        items[mine, OFF_X:OFF_Y + 1] = offsets[:, v, :]
        items[mine, LIVE:LIVE + 1] = turned[0:count, views:views + 1]
        items[mine, VIEW:VIEW + 1] = jnp.full((count, 1), v, jnp.int32)
        items[mine, ABSORB:ABSORB + 1] = turned[0:count, views + 1:views + 2]
        items[mine, TILE:TILE + 1] = targets[:, v:v + 1]
        items[mine, RANK:RANK + 1] = turned[0:count, v:v + 1]
        items[mine, BRICK:BRICK + 1] = lax.broadcasted_iota(jnp.int32, (count, 1), 0)
    me = lax.broadcasted_iota(jnp.int32, (size, size), 0)
    it = lax.broadcasted_iota(jnp.int32, (size, size), 1)
    used = views * count
    owner = jnp.where(me < used, lax.rem(lax.div(items[:, TILE:TILE + 1], 2), row), -1)
    same = (owner == owner.T) & (it < me)
    slot = owner * capacity + jnp.sum(jnp.where(same, 1, 0), axis=1, keepdims=True)
    slot = jnp.where(me < used, slot, -1)
    chosen_v[0:1, :] = jnp.sum(
        jnp.where(slot == it, items[:, BRICK:BRICK + 1], 0), axis=0, keepdims=True
    )
    load_chosen = pltpu.make_async_copy(chosen_v, chosen_s, local_sem.at[1])
    load_chosen.start()
    hit = (slot.T == me)[0:slots, :]
    lane = lax.broadcasted_iota(jnp.int32, (slots, LANES), 1)
    table = jnp.where(lane == TILE, -1, 0)
    entry = jnp.where(lane[0:1, :] == TILE, lax.rem(items[...], 2) + 1, items[...])
    hit_int = jnp.where(hit, 1, 0)
    for i in range(used):
        table = table + hit_int[:, i:i + 1] * entry[i:i + 1, :]
    for d in range(row):
        send_table[d, 0:capacity, :] = table[d * capacity:(d + 1) * capacity, :]

    def table_copy(e, py, pz):
        return pltpu.make_async_remote_copy(
            src_ref=send_table.at[py * nz + pz], dst_ref=recv_table.at[e],
            send_sem=table_send.at[e], recv_sem=table_recv.at[e],
            device_id={"gy": py, "gz": pz}, device_id_type=MESH,
        )

    def brick_copy(e, py, pz):
        return pltpu.make_async_remote_copy(
            src_ref=send_buf.at[e], dst_ref=recv_buf.at[e],
            send_sem=brick_send.at[e], recv_sem=brick_recv.at[e],
            device_id={"gy": py, "gz": pz}, device_id_type=MESH,
        )

    def relay_copy(dy, dz, py, pz):
        return pltpu.make_async_remote_copy(
            src_ref=relay_buf.at[dy], dst_ref=recv_buf.at[dz * ny + dy],
            send_sem=relay_send.at[dy], recv_sem=brick_recv.at[dz * ny + dy],
            device_id={"gy": py, "gz": pz}, device_id_type=MESH,
        )

    def gather(source, chosen, py, pz, into, e):
        for c in range(capacity):
            into[e, c] = source[chosen[0, (py * nz + pz) * capacity + c]]

    def send(dy, dz):
        def direct():
            e = dz * ny + dy
            py, pz = peer(dy, dz)
            gather(bricks, chosen_s, py, pz, send_buf, e)
            brick_copy(e, py, pz).start()

        if relayed:
            pl.when(jnp.logical_not(leaves_raw(dz)))(direct)
        else:
            direct()

    pieces = ny if count % ny == 0 else 1
    depth = count // pieces
    partner = 2 * half - 1 - my_z
    beyond = jnp.where(upper, half + 1, half - 2)

    def raw_copy(j, source, sent, pz):
        part = pl.ds(j * depth, depth)
        return pltpu.make_async_remote_copy(
            src_ref=source.at[part], dst_ref=raw_buf.at[part],
            send_sem=sent.at[j], recv_sem=raw_recv.at[j],
            device_id={"gy": my_y, "gz": pz}, device_id_type=MESH,
        )

    def raw_chosen_copy(source, sent, pz):
        return pltpu.make_async_remote_copy(
            src_ref=source, dst_ref=raw_chosen_v,
            send_sem=sent.at[pieces], recv_sem=raw_recv.at[pieces],
            device_id={"gy": my_y, "gz": pz}, device_id_type=MESH,
        )

    load_bricks.wait()
    load_chosen.wait()
    pl.semaphore_wait(barrier, row - 1)
    if relayed:
        @pl.when(inner)
        def _():
            raw_copy(0, bricks, raw_send, partner).start()
            raw_chosen_copy(chosen_v, raw_send, partner).start()

    for e in range(1, row):
        table_copy(e, *peer(e % ny, e // ny)).start()
    for dy in range(ny):
        send(dy, go(1))
        if dy:
            send(dy, jnp.int32(0))
        if relayed and 0 < dy < pieces:
            @pl.when(inner)
            def _():
                raw_copy(dy, bricks, raw_send, partner).start()

    for t in range(2, nz):
        for dy in range(ny):
            send(dy, go(t))

    gather(bricks, chosen_s, my_y, my_z, recv_buf, 0)
    recv_table[0] = send_table[my_y * nz + my_z]
    rows = lax.broadcasted_iota(jnp.int32, (extent, extent), 0)
    cols = lax.broadcasted_iota(jnp.int32, (extent, extent), 1)
    spacing[...] = (rows - cols).astype(F32)

    def table_arrived(e, _):
        table_copy(e, my_y, my_z).wait_recv()
        return 0

    lax.fori_loop(1, row, table_arrived, 0)
    keys[...] = jnp.full(keys.shape, -1, jnp.int32)
    for e in range(row):
        keys[e * capacity:(e + 1) * capacity, :] = recv_table[e, 0:capacity, :]
    view = keys[:, VIEW:VIEW + 1]
    for axis in range(2):
        slope = jnp.zeros((size, 1), F32)
        for v in range(views):
            slope = jnp.where(view == v, shear[v:v + 1, axis:axis + 1], slope)
        offset = keys[:, OFF_X + axis:OFF_X + axis + 1].astype(F32)
        for k in range(layers):
            shift_v[:, 3 * k + axis:3 * k + axis + 1] = offset + float(k - layers // 2) * slope
    strength = keys[:, ABSORB:ABSORB + 1].astype(F32) * (1.0 / ABSORB_UNIT)
    for k in range(layers):
        shift_v[:, 3 * k + 2:3 * k + 3] = jnp.where(keys[:, LIVE:LIVE + 1] > k, strength, 0.0)
    to_shift = pltpu.make_async_copy(shift_v, shift_s, local_sem.at[3])
    to_shift.start()
    tile = keys[:, TILE:TILE + 1]
    key = jnp.where(tile < 0, 2, tile) * (1 << 20) + keys[:, RANK:RANK + 1]
    key = jnp.broadcast_to(key, (size, size))
    other = key.T
    ahead = (other < key) | ((other == key) & (it < me))
    place = jnp.sum(jnp.where(ahead, 1, 0), axis=1, keepdims=True)
    hit = place == it
    sort_v[0:1, :] = jnp.sum(jnp.where(hit, me, 0), axis=0, keepdims=True)
    sort_v[1:2, :] = jnp.sum(jnp.where(hit & (tile == 0), 1, 0), axis=0, keepdims=True)
    sort_v[2:3, :] = jnp.sum(jnp.where(hit & (tile == 1), 1, 0), axis=0, keepdims=True)
    to_sort = pltpu.make_async_copy(sort_v, sort_s, local_sem.at[2])
    to_sort.start()
    to_shift.wait()
    to_sort.wait()

    def interp(distance):
        return jnp.maximum(0.0, 1.0 - jnp.abs(distance)).astype(BF16)

    strip_rows = 32

    def render(e):
        spots = [e * capacity + c for c in range(capacity)]
        for c in range(capacity):
            for k in range(layers):
                across = interp(spacing[...] - shift_s[spots[c], 3 * k])
                downward_t = interp(spacing[...] + shift_s[spots[c], 3 * k + 1])
                halfway = jnp.dot(across, recv_buf[e, c, k], preferred_element_type=F32).astype(BF16)
                dense[c, k] = jnp.dot(halfway, downward_t, preferred_element_type=F32)
        for c in range(capacity):
            for begin in range(0, extent, strip_rows):
                lines = slice(begin, begin + strip_rows)
                optical, clear, colors = None, None, [None] * 3
                for k in range(layers):
                    density = dense[c, k, lines, :]
                    rate = shift_s[spots[c], 3 * k + 2]
                    soft = jnp.maximum(density, 0.0) + jnp.log(1.0 + jnp.exp(-jnp.abs(density)))
                    thickness = rate * soft
                    passed = jnp.exp(-thickness)
                    half_alpha = 0.5 - 0.5 * passed
                    if k:
                        half_alpha = half_alpha * clear
                    for n in range(3):
                        lit = half_alpha + half_alpha * jnp.tanh(
                            (0.5 * gain[n]) * density + 0.5 * bias[n]
                        )
                        colors[n] = lit if k == 0 else colors[n] + lit
                    optical = thickness if k == 0 else optical + thickness
                    clear = passed if k == 0 else clear * passed
                for n in range(3):
                    foot[spots[c], n, lines, :] = colors[n].astype(BF16)
                foot[spots[c], 3, lines, :] = optical.astype(BF16)

    def arrived(e):
        brick_copy(e, my_y, my_z).wait_recv()

    def plain(first, dz):
        def step(dy, _):
            arrived(dz * ny + dy)
            render(dz * ny + dy)
            return 0

        lax.fori_loop(first, ny, step, 0)

    render(jnp.int32(0))
    plain(1, jnp.int32(0))
    for t in range(1, nz):
        dz = come(t)
        if relayed and t == 1:
            @pl.when(inner)
            def _():
                raw_chosen_copy(chosen_v, raw_send, partner).wait_recv()
                raw_chosen_copy(raw_chosen_v, forward_send, beyond).start()

            def step(dy, _):
                @pl.when(inner & (dy < pieces))
                def _():
                    raw_copy(dy, bricks, raw_send, partner).wait_recv()
                    raw_copy(dy, raw_buf, forward_send, beyond).start()

                arrived(dz * ny + dy)
                render(dz * ny + dy)
                return 0

            lax.fori_loop(0, ny, step, 0)
        elif relayed and t == 2:
            @pl.when(holder)
            def _():
                @pl.when(jnp.logical_not(inner))
                def _():
                    raw_chosen_copy(chosen_v, raw_send, partner).wait_recv()
                    for j in range(pieces):
                        raw_copy(j, bricks, raw_send, partner).wait_recv()

                load_raw_chosen = pltpu.make_async_copy(raw_chosen_v, raw_chosen_s, local_sem.at[4])
                load_raw_chosen.start()
                load_raw_chosen.wait()
                for dy in range(1, ny):
                    py, pz = peer(dy, 0)
                    gather(raw_buf, raw_chosen_s, py, pz, relay_buf, dy)
                    relay_copy(dy, dz, py, pz).start()
                gather(raw_buf, raw_chosen_s, my_y, my_z, recv_buf, dz * ny)

            @pl.when(jnp.logical_not(holder))
            def _():
                arrived(dz * ny)

            render(dz * ny)
            plain(1, dz)
        else:
            plain(0, dz)

    def left(e, _):
        table_copy(e, my_y, my_z).wait_send()

        def direct():
            brick_copy(e, my_y, my_z).wait_send()

        if relayed:
            pl.when(jnp.logical_not(leaves_raw(lax.div(e, ny))))(direct)
        else:
            direct()
        return 0

    lax.fori_loop(1, row, left, 0)
    if relayed:
        @pl.when(inner)
        def _():
            for j in range(pieces):
                raw_copy(j, bricks, raw_send, partner).wait_send()
                raw_copy(j, raw_buf, forward_send, beyond).wait_send()
            raw_chosen_copy(chosen_v, raw_send, partner).wait_send()
            raw_chosen_copy(raw_chosen_v, forward_send, beyond).wait_send()

        @pl.when(holder)
        def _():
            for dy in range(1, ny):
                relay_copy(dy, jnp.int32(0), my_y, my_z).wait_send()

    height = 16

    def strip(r, _):
        lines = pl.ds(pl.multiple_of(r * height, height), height)

        def visit(p, carry):
            optical0, optical1, color0, color1 = carry
            which = sort_s[0, p]
            in0 = sort_s[1, p].astype(F32)
            in1 = sort_s[2, p].astype(F32)
            clear = jnp.exp(-(optical0 * in0 + optical1 * in1))
            clear0, clear1 = clear * in0, clear * in1
            shade = [foot[which, n, lines, :].astype(F32) for n in range(3)]
            depth = foot[which, 3, lines, :].astype(F32)
            return (
                optical0 + in0 * depth,
                optical1 + in1 * depth,
                tuple(c + clear0 * s for c, s in zip(color0, shade)),
                tuple(c + clear1 * s for c, s in zip(color1, shade)),
            )

        zero = jnp.zeros((height, extent), F32)
        optical0, optical1, color0, color1 = lax.fori_loop(
            0, slots, visit, (zero, zero, (zero,) * 3, (zero,) * 3), unroll=4
        )
        for n in range(3):
            out[0, n, lines, :] = color0[n]
            out[1, n, lines, :] = color1[n]
        out[0, 3, lines, :] = jnp.exp(-optical0)
        out[1, 3, lines, :] = jnp.exp(-optical1)
        return 0

    lax.fori_loop(0, extent // height, strip, 0)


def body(ny, nz, bricks, live, shear, offsets, absorb, color_gain, color_bias, targets, order):
    brick_count, layers, extent, _ = bricks.shape
    views = shear.shape[0]
    row = ny * nz
    capacity = (brick_count * views + row - 1) // row
    slots = row * capacity
    smem = pl.BlockSpec(memory_space=pltpu.SMEM)
    vmem = pl.BlockSpec(memory_space=pltpu.VMEM)
    table_rows = (capacity + 7) // 8 * 8
    longest = max(slots, brick_count * views)
    size = (longest + LANES - 1) // LANES * LANES
    return pl.pallas_call(
        functools.partial(main_kernel, ny, nz, capacity),
        out_shape=jax.ShapeDtypeStruct((2, 4, extent, extent), F32),
        in_specs=[pl.BlockSpec(memory_space=pl.ANY), vmem, vmem, vmem, vmem, smem, smem, vmem, vmem],
        out_specs=vmem,
        scratch_shapes=[
            pltpu.VMEM(bricks.shape, BF16),
            pltpu.VMEM(bricks.shape, BF16),
            pltpu.VMEM((ny, capacity, layers, extent, extent), BF16),
            pltpu.VMEM((8, size), jnp.int32),
            pltpu.SMEM((8, size), jnp.int32),
            pltpu.VMEM((row, capacity, layers, extent, extent), BF16),
            pltpu.VMEM((row, capacity, layers, extent, extent), BF16),
            pltpu.VMEM((row, table_rows, LANES), jnp.int32),
            pltpu.VMEM((row, table_rows, LANES), jnp.int32),
            pltpu.VMEM((LANES, LANES), jnp.int32),
            pltpu.VMEM((size, LANES), jnp.int32),
            pltpu.VMEM((8, size), jnp.int32),
            pltpu.SMEM((8, size), jnp.int32),
            pltpu.VMEM((size, LANES), F32),
            pltpu.SMEM((size, LANES), F32),
            pltpu.VMEM((8, size), jnp.int32),
            pltpu.SMEM((8, size), jnp.int32),
            pltpu.VMEM((extent, extent), F32),
            pltpu.VMEM((capacity, layers, extent, extent), F32),
            pltpu.VMEM((slots, 4, extent, extent), BF16),
            pltpu.VMEM((size, LANES), jnp.int32),
            pltpu.SemaphoreType.DMA((row,)),
            pltpu.SemaphoreType.DMA((row,)),
            pltpu.SemaphoreType.DMA((row,)),
            pltpu.SemaphoreType.DMA((row,)),
            pltpu.SemaphoreType.DMA((ny + 1,)),
            pltpu.SemaphoreType.DMA((ny + 1,)),
            pltpu.SemaphoreType.DMA((ny + 1,)),
            pltpu.SemaphoreType.DMA((ny,)),
            pltpu.SemaphoreType.DMA((5,)),
        ],
        compiler_params=pltpu.CompilerParams(
            collective_id=0, has_side_effects=True, vmem_limit_bytes=48 * 1024 * 1024
        ),
    )(
        bricks, live.reshape(1, brick_count), shear, offsets, absorb.reshape(1, brick_count),
        color_gain, color_bias, targets, order,
    )


def solution(mesh):
    ny, nz = mesh.shape["gy"], mesh.shape["gz"]
    split = ("gx", "gy", "gz")
    placed = (
        P(split, None, None, None),
        P(split),
        P(),
        P(split, None, None),
        P(split),
        P(),
        P(),
        P(split, None),
        P(None, split),
    )
    return jax.shard_map(
        functools.partial(body, ny, nz),
        mesh=mesh,
        in_specs=placed,
        out_specs=P(split, None, None, None),
        check_vma=False,
    )
```

```python
import functools

import jax
import jax.numpy as jnp
from jax import lax
from jax.experimental import pallas as pl
from jax.experimental.pallas import tpu as pltpu
from jax.sharding import PartitionSpec as P

MESH = pl.DeviceIdType.MESH
F32 = jnp.float32
BF16 = jnp.bfloat16
LANES = 128
ABSORB_UNIT = float(2**20)
OFF_X, OFF_Y, LIVE, VIEW, ABSORB, TILE, RANK, BRICK = range(8)


def main_kernel(
    ny, nz, capacity,
    bricks_in, live, shear, offsets, absorb, gain, bias, targets, order,
    out,
    bricks, column_v, column_s, send_buf, recv_buf, send_table, recv_table, raw, items, chosen_v, chosen_s,
    shift_v, shift_s, sort_v, sort_s, spacing, dense, foot, keys,
    table_send, table_recv, brick_send, brick_recv, column_send, column_recv, block_send, block_recv,
    local_sem, *blocks,
):
    row = ny * nz
    slots = row * capacity
    count, layers, extent, _ = bricks.shape
    views = targets.shape[1]
    size = keys.shape[0]
    my_y, my_z = lax.axis_index("gy"), lax.axis_index("gz")
    way_to = (my_z + 1, my_z - 1)
    has_next = (my_z + 1 < nz, my_z >= 1)

    def exists(way, d):
        return my_z >= d if way == 0 else my_z + d < nz

    def step_of(way, d):
        return d if way == 0 else nz - d

    def held(way, d):
        return blocks[way * (nz - 1) + d - 1] if d else bricks

    def peer(dy, dz):
        return lax.rem(my_y + dy, ny), lax.rem(my_z + dz, nz)

    barrier = pltpu.get_barrier_semaphore()
    for e in range(1, row):
        py, pz = peer(e % ny, e // ny)
        pl.semaphore_signal(barrier, inc=1, device_id={"gy": py, "gz": pz}, device_id_type=MESH)

    load_bricks = pltpu.make_async_copy(bricks_in, bricks, local_sem.at[0])
    load_bricks.start()

    raw[...] = jnp.zeros(raw.shape, jnp.int32)
    raw[0:views, 0:count] = order[...]
    raw[views:views + 1, 0:count] = live[...]
    units = jnp.round(absorb[...].astype(F32) * ABSORB_UNIT)
    raw[views + 1:views + 2, 0:count] = units.astype(jnp.int32)
    turned = raw[...].T
    items[...] = jnp.zeros(items.shape, jnp.int32)
    for v in range(views):
        mine = slice(v * count, (v + 1) * count)
        items[mine, OFF_X:OFF_Y + 1] = offsets[:, v, :]
        items[mine, LIVE:LIVE + 1] = turned[0:count, views:views + 1]
        items[mine, VIEW:VIEW + 1] = jnp.full((count, 1), v, jnp.int32)
        items[mine, ABSORB:ABSORB + 1] = turned[0:count, views + 1:views + 2]
        items[mine, TILE:TILE + 1] = targets[:, v:v + 1]
        items[mine, RANK:RANK + 1] = turned[0:count, v:v + 1]
        items[mine, BRICK:BRICK + 1] = lax.broadcasted_iota(jnp.int32, (count, 1), 0)
    me = lax.broadcasted_iota(jnp.int32, (size, size), 0)
    it = lax.broadcasted_iota(jnp.int32, (size, size), 1)
    used = views * count
    owner = jnp.where(me < used, lax.rem(lax.div(items[:, TILE:TILE + 1], 2), row), -1)
    same = (owner == owner.T) & (it < me)
    slot = owner * capacity + jnp.sum(jnp.where(same, 1, 0), axis=1, keepdims=True)
    slot = jnp.where(me < used, slot, -1)
    chosen_v[0:1, :] = jnp.sum(
        jnp.where(slot == it, items[:, BRICK:BRICK + 1], 0), axis=0, keepdims=True
    )
    load_chosen = pltpu.make_async_copy(chosen_v, chosen_s, local_sem.at[1])
    load_chosen.start()
    hit = (slot.T == me)[0:slots, :]
    lane = lax.broadcasted_iota(jnp.int32, (slots, LANES), 1)
    table = jnp.where(lane == TILE, -1, 0)
    entry = jnp.where(lane[0:1, :] == TILE, lax.rem(items[...], 2) + 1, items[...])
    hit_int = jnp.where(hit, 1, 0)
    for i in range(used):
        table = table + hit_int[:, i:i + 1] * entry[i:i + 1, :]
    for d in range(row):
        send_table[d, 0:capacity, :] = table[d * capacity:(d + 1) * capacity, :]

    def table_copy(e, py, pz):
        return pltpu.make_async_remote_copy(
            src_ref=send_table.at[py * nz + pz], dst_ref=recv_table.at[e],
            send_sem=table_send.at[e], recv_sem=table_recv.at[e],
            device_id={"gy": py, "gz": pz}, device_id_type=MESH,
        )

    def brick_copy(e, py, pz):
        return pltpu.make_async_remote_copy(
            src_ref=send_buf.at[e], dst_ref=recv_buf.at[e],
            send_sem=brick_send.at[e], recv_sem=brick_recv.at[e],
            device_id={"gy": py, "gz": pz}, device_id_type=MESH,
        )

    def gather(source, chosen, py, pz, into, e):
        for c in range(capacity):
            into[e, c] = source[chosen[(py * nz + pz) * capacity + c]]

    pieces = ny if count % ny == 0 else 1
    depth = count // pieces

    def block_copy(way, d, j):
        part = pl.ds(j * depth, depth)
        return pltpu.make_async_remote_copy(
            src_ref=held(way, d).at[part], dst_ref=held(way, d + 1).at[part],
            send_sem=block_send.at[(way * nz + d) * pieces + j],
            recv_sem=block_recv.at[(way * nz + d + 1) * pieces + j],
            device_id={"gy": my_y, "gz": way_to[way]}, device_id_type=MESH,
        )

    def column_copy(dz, pz):
        return pltpu.make_async_remote_copy(
            src_ref=chosen_v, dst_ref=column_v.at[dz],
            send_sem=column_send.at[dz], recv_sem=column_recv.at[dz],
            device_id={"gy": my_y, "gz": pz}, device_id_type=MESH,
        )

    def offer(way, d, j):
        @pl.when(exists(way, d) & has_next[way])
        def _():
            block_copy(way, d, j).start()

    def share(block, chosen, dz, dy):
        py, pz = peer(dy, 0)
        gather(block, chosen, py, pz, send_buf, dz * ny + dy)
        brick_copy(dz * ny + dy, py, pz).start()

    load_bricks.wait()
    load_chosen.wait()
    pl.semaphore_wait(barrier, row - 1)
    for way in range(2):
        offer(way, 0, 0)
    for dz in range(1, nz):
        column_copy(dz, lax.rem(my_z + dz, nz)).start()
    for e in range(1, row):
        table_copy(e, *peer(e % ny, e // ny)).start()
    for j in range(1, max(ny, pieces)):
        if j < pieces:
            for way in range(2):
                offer(way, 0, j)
        if j < ny:
            share(bricks, chosen_s.at[0], 0, j)

    gather(bricks, chosen_s.at[0], my_y, my_z, recv_buf, 0)
    column_v[0] = chosen_v[...]
    recv_table[0] = send_table[my_y * nz + my_z]
    rows = lax.broadcasted_iota(jnp.int32, (extent, extent), 0)
    cols = lax.broadcasted_iota(jnp.int32, (extent, extent), 1)
    spacing[...] = (rows - cols).astype(F32)

    def table_arrived(e, _):
        table_copy(e, my_y, my_z).wait_recv()
        return 0

    lax.fori_loop(1, row, table_arrived, 0)
    for dz in range(1, nz):
        column_copy(dz, my_z).wait_recv()
    load_column = pltpu.make_async_copy(column_v, column_s, local_sem.at[4])
    load_column.start()
    keys[...] = jnp.full(keys.shape, -1, jnp.int32)
    for e in range(row):
        keys[e * capacity:(e + 1) * capacity, :] = recv_table[e, 0:capacity, :]
    view = keys[:, VIEW:VIEW + 1]
    for axis in range(2):
        slope = jnp.zeros((size, 1), F32)
        for v in range(views):
            slope = jnp.where(view == v, shear[v:v + 1, axis:axis + 1], slope)
        offset = keys[:, OFF_X + axis:OFF_X + axis + 1].astype(F32)
        for k in range(layers):
            shift_v[:, 3 * k + axis:3 * k + axis + 1] = offset + float(k - layers // 2) * slope
    strength = keys[:, ABSORB:ABSORB + 1].astype(F32) * (1.0 / ABSORB_UNIT)
    for k in range(layers):
        shift_v[:, 3 * k + 2:3 * k + 3] = jnp.where(keys[:, LIVE:LIVE + 1] > k, strength, 0.0)
    to_shift = pltpu.make_async_copy(shift_v, shift_s, local_sem.at[3])
    to_shift.start()
    tile = keys[:, TILE:TILE + 1]
    key = jnp.where(tile < 0, 2, tile) * (1 << 20) + keys[:, RANK:RANK + 1]
    key = jnp.broadcast_to(key, (size, size))
    other = key.T
    ahead = (other < key) | ((other == key) & (it < me))
    place = jnp.sum(jnp.where(ahead, 1, 0), axis=1, keepdims=True)
    hit = place == it
    sort_v[0:1, :] = jnp.sum(jnp.where(hit, me, 0), axis=0, keepdims=True)
    sort_v[1:2, :] = jnp.sum(jnp.where(hit & (tile == 0), 1, 0), axis=0, keepdims=True)
    sort_v[2:3, :] = jnp.sum(jnp.where(hit & (tile == 1), 1, 0), axis=0, keepdims=True)
    to_sort = pltpu.make_async_copy(sort_v, sort_s, local_sem.at[2])
    to_sort.start()
    to_shift.wait()
    to_sort.wait()
    load_column.wait()

    def interp(distance):
        return jnp.maximum(0.0, 1.0 - jnp.abs(distance)).astype(BF16)

    strip_rows = 32

    def render(e):
        spots = [e * capacity + c for c in range(capacity)]
        for c in range(capacity):
            for k in range(layers):
                across = interp(spacing[...] - shift_s[spots[c], 3 * k])
                downward_t = interp(spacing[...] + shift_s[spots[c], 3 * k + 1])
                halfway = jnp.dot(across, recv_buf[e, c, k], preferred_element_type=F32).astype(BF16)
                dense[c, k] = jnp.dot(halfway, downward_t, preferred_element_type=F32)
        for c in range(capacity):
            for begin in range(0, extent, strip_rows):
                lines = slice(begin, begin + strip_rows)
                optical, clear, colors = None, None, [None] * 3
                for k in range(layers):
                    density = dense[c, k, lines, :]
                    rate = shift_s[spots[c], 3 * k + 2]
                    soft = jnp.maximum(density, 0.0) + jnp.log(1.0 + jnp.exp(-jnp.abs(density)))
                    thickness = rate * soft
                    passed = jnp.exp(-thickness)
                    half_alpha = 0.5 - 0.5 * passed
                    if k:
                        half_alpha = half_alpha * clear
                    for n in range(3):
                        lit = half_alpha + half_alpha * jnp.tanh(
                            (0.5 * gain[n]) * density + 0.5 * bias[n]
                        )
                        colors[n] = lit if k == 0 else colors[n] + lit
                    optical = thickness if k == 0 else optical + thickness
                    clear = passed if k == 0 else clear * passed
                for n in range(3):
                    foot[spots[c], n, lines, :] = colors[n].astype(BF16)
                foot[spots[c], 3, lines, :] = optical.astype(BF16)

    for d in range(nz):
        below = exists(0, d)
        number = jnp.int32(1) if d == 0 else below.astype(jnp.int32) + exists(1, d).astype(jnp.int32)

        def entry(i, _):
            if d + 1 < nz:
                for way in range(2):
                    @pl.when(exists(way, d + 1) & (i < pieces))
                    def _():
                        block_copy(way, d, i).wait_recv()
                        if d + 2 < nz:
                            offer(way, d + 1, i)

            dz = jnp.where((i < ny) & below, d, nz - d)
            e = dz * ny + lax.rem(i, ny)

            @pl.when(lax.rem(i, ny) > 0)
            def _():
                brick_copy(e, my_y, my_z).wait_recv()

            render(e)
            return 0

        lax.fori_loop(0, number * ny, entry, 0)
        if d + 1 < nz:
            for way in range(2):
                @pl.when(exists(way, d + 1))
                def _():
                    dz = step_of(way, d + 1)
                    for dy in range(1, ny):
                        share(held(way, d + 1), column_s.at[dz, 0], dz, dy)
                    gather(held(way, d + 1), column_s.at[dz, 0], my_y, my_z, recv_buf, dz * ny)

    def left(e, _):
        table_copy(e, my_y, my_z).wait_send()

        @pl.when(lax.rem(e, ny) > 0)
        def _():
            brick_copy(e, my_y, my_z).wait_send()

        return 0

    lax.fori_loop(1, row, left, 0)
    for dz in range(1, nz):
        column_copy(dz, my_z).wait_send()
    for way in range(2):
        for d in range(nz - 1):
            @pl.when(exists(way, d) & has_next[way])
            def _():
                for j in range(pieces):
                    block_copy(way, d, j).wait_send()

    height = 16

    def strip(r, _):
        lines = pl.ds(pl.multiple_of(r * height, height), height)

        def visit(p, carry):
            optical0, optical1, color0, color1 = carry
            which = sort_s[0, p]
            in0 = sort_s[1, p].astype(F32)
            in1 = sort_s[2, p].astype(F32)
            clear = jnp.exp(-(optical0 * in0 + optical1 * in1))
            clear0, clear1 = clear * in0, clear * in1
            shade = [foot[which, n, lines, :].astype(F32) for n in range(3)]
            depth = foot[which, 3, lines, :].astype(F32)
            return (
                optical0 + in0 * depth,
                optical1 + in1 * depth,
                tuple(c + clear0 * s for c, s in zip(color0, shade)),
                tuple(c + clear1 * s for c, s in zip(color1, shade)),
            )

        zero = jnp.zeros((height, extent), F32)
        optical0, optical1, color0, color1 = lax.fori_loop(
            0, slots, visit, (zero, zero, (zero,) * 3, (zero,) * 3), unroll=4
        )
        for n in range(3):
            out[0, n, lines, :] = color0[n]
            out[1, n, lines, :] = color1[n]
        out[0, 3, lines, :] = jnp.exp(-optical0)
        out[1, 3, lines, :] = jnp.exp(-optical1)
        return 0

    lax.fori_loop(0, extent // height, strip, 0)


def body(ny, nz, bricks, live, shear, offsets, absorb, color_gain, color_bias, targets, order):
    brick_count, layers, extent, _ = bricks.shape
    views = shear.shape[0]
    row = ny * nz
    capacity = (brick_count * views + row - 1) // row
    slots = row * capacity
    smem = pl.BlockSpec(memory_space=pltpu.SMEM)
    vmem = pl.BlockSpec(memory_space=pltpu.VMEM)
    table_rows = (capacity + 7) // 8 * 8
    longest = max(slots, brick_count * views)
    size = (longest + LANES - 1) // LANES * LANES
    return pl.pallas_call(
        functools.partial(main_kernel, ny, nz, capacity),
        out_shape=jax.ShapeDtypeStruct((2, 4, extent, extent), F32),
        in_specs=[pl.BlockSpec(memory_space=pl.ANY), vmem, vmem, vmem, vmem, smem, smem, vmem, vmem],
        out_specs=vmem,
        scratch_shapes=[
            pltpu.VMEM(bricks.shape, BF16),
            pltpu.VMEM((nz, 8, size), jnp.int32),
            pltpu.SMEM((nz, 8, size), jnp.int32),
            pltpu.VMEM((row, capacity, layers, extent, extent), BF16),
            pltpu.VMEM((row, capacity, layers, extent, extent), BF16),
            pltpu.VMEM((row, table_rows, LANES), jnp.int32),
            pltpu.VMEM((row, table_rows, LANES), jnp.int32),
            pltpu.VMEM((LANES, LANES), jnp.int32),
            pltpu.VMEM((size, LANES), jnp.int32),
            pltpu.VMEM((8, size), jnp.int32),
            pltpu.SMEM((8, size), jnp.int32),
            pltpu.VMEM((size, LANES), F32),
            pltpu.SMEM((size, LANES), F32),
            pltpu.VMEM((8, size), jnp.int32),
            pltpu.SMEM((8, size), jnp.int32),
            pltpu.VMEM((extent, extent), F32),
            pltpu.VMEM((capacity, layers, extent, extent), F32),
            pltpu.VMEM((slots, 4, extent, extent), BF16),
            pltpu.VMEM((size, LANES), jnp.int32),
            pltpu.SemaphoreType.DMA((row,)),
            pltpu.SemaphoreType.DMA((row,)),
            pltpu.SemaphoreType.DMA((row,)),
            pltpu.SemaphoreType.DMA((row,)),
            pltpu.SemaphoreType.DMA((nz,)),
            pltpu.SemaphoreType.DMA((nz,)),
            pltpu.SemaphoreType.DMA((2 * nz * ny,)),
            pltpu.SemaphoreType.DMA((2 * nz * ny,)),
            pltpu.SemaphoreType.DMA((5,)),
            *[pltpu.VMEM(bricks.shape, BF16) for _ in range(2 * (nz - 1))],
        ],
        compiler_params=pltpu.CompilerParams(
            collective_id=0, has_side_effects=True, vmem_limit_bytes=48 * 1024 * 1024
        ),
    )(
        bricks, live.reshape(1, brick_count), shear, offsets, absorb.reshape(1, brick_count),
        color_gain, color_bias, targets, order,
    )


def solution(mesh):
    ny, nz = mesh.shape["gy"], mesh.shape["gz"]
    split = ("gx", "gy", "gz")
    placed = (
        P(split, None, None, None),
        P(split),
        P(),
        P(split, None, None),
        P(split),
        P(),
        P(),
        P(split, None),
        P(None, split),
    )
    return jax.shard_map(
        functools.partial(body, ny, nz),
        mesh=mesh,
        in_specs=placed,
        out_specs=P(split, None, None, None),
        check_vma=False,
    )
```

```python
import functools

import jax
import jax.numpy as jnp
from jax import lax
from jax.experimental import pallas as pl
from jax.experimental.pallas import tpu as pltpu
from jax.sharding import PartitionSpec as P

MESH = pl.DeviceIdType.MESH
F32 = jnp.float32
BF16 = jnp.bfloat16
LANES = 128
ABSORB_UNIT = float(2**20)
OFF_X, OFF_Y, LIVE, VIEW, ABSORB, TILE, RANK, BRICK = range(8)


def main_kernel(
    ny, nz, capacity,
    bricks_in, live_in, shear_in, offsets_in, absorb_in, gain, bias, targets_in, order_in,
    out,
    bricks, column_v, column_s, send_buf, recv_buf, send_table, recv_table, raw, items, chosen_v, chosen_s,
    shift_v, shift_s, sort_v, sort_s, spacing, dense, foot, keys,
    table_send, table_recv, brick_send, brick_recv, column_send, column_recv, block_send, block_recv,
    far_buf, far_send, local_sem, live, shear, offsets, absorb, targets, order, *blocks,
):
    row = ny * nz
    slots = row * capacity
    count, layers, extent, _ = bricks_in.shape
    views = targets_in.shape[1]
    size = keys.shape[0]
    my_y, my_z = lax.axis_index("gy"), lax.axis_index("gz")
    way_to = (my_z + 1, my_z - 1)
    has_next = (my_z + 1 < nz, my_z >= 1)

    def exists(way, d):
        return my_z >= d if way == 0 else my_z + d < nz

    def step_of(way, d):
        return d if way == 0 else nz - d

    whole = nz - 1 if nz >= 3 else nz

    def held(way, d):
        return blocks[way * (nz - 1) + d - 1] if d else bricks

    def peer(dy, dz):
        return lax.rem(my_y + dy, ny), lax.rem(my_z + dz, nz)

    barrier = pltpu.get_barrier_semaphore()
    for e in range(1, row):
        py, pz = peer(e % ny, e // ny)
        pl.semaphore_signal(barrier, inc=1, device_id={"gy": py, "gz": pz}, device_id_type=MESH)

    load_bricks = pltpu.make_async_copy(bricks_in, bricks, local_sem.at[0])
    loads = [
        pltpu.make_async_copy(source, into, local_sem.at[5 + n])
        for n, (source, into) in enumerate((
            (live_in, live), (shear_in, shear), (offsets_in, offsets),
            (absorb_in, absorb), (targets_in, targets), (order_in, order),
        ))
    ]
    for load in loads:
        load.start()
    load_bricks.start()
    for load in loads:
        load.wait()

    raw[...] = jnp.zeros(raw.shape, jnp.int32)
    raw[0:views, 0:count] = order[...]
    raw[views:views + 1, 0:count] = live[...]
    units = jnp.round(absorb[...].astype(F32) * ABSORB_UNIT)
    raw[views + 1:views + 2, 0:count] = units.astype(jnp.int32)
    turned = raw[...].T
    items[...] = jnp.zeros(items.shape, jnp.int32)
    for v in range(views):
        mine = slice(v * count, (v + 1) * count)
        items[mine, OFF_X:OFF_Y + 1] = offsets[:, v, :]
        items[mine, LIVE:LIVE + 1] = turned[0:count, views:views + 1]
        items[mine, VIEW:VIEW + 1] = jnp.full((count, 1), v, jnp.int32)
        items[mine, ABSORB:ABSORB + 1] = turned[0:count, views + 1:views + 2]
        items[mine, TILE:TILE + 1] = targets[:, v:v + 1]
        items[mine, RANK:RANK + 1] = turned[0:count, v:v + 1]
        items[mine, BRICK:BRICK + 1] = lax.broadcasted_iota(jnp.int32, (count, 1), 0)
    me = lax.broadcasted_iota(jnp.int32, (size, size), 0)
    it = lax.broadcasted_iota(jnp.int32, (size, size), 1)
    used = views * count
    owner = jnp.where(me < used, lax.rem(lax.div(items[:, TILE:TILE + 1], 2), row), -1)
    same = (owner == owner.T) & (it < me)
    slot = owner * capacity + jnp.sum(jnp.where(same, 1, 0), axis=1, keepdims=True)
    slot = jnp.where(me < used, slot, -1)
    chosen_v[0:1, :] = jnp.sum(
        jnp.where(slot == it, items[:, BRICK:BRICK + 1], 0), axis=0, keepdims=True
    )
    load_chosen = pltpu.make_async_copy(chosen_v, chosen_s, local_sem.at[1])
    load_chosen.start()
    hit = (slot.T == me)[0:slots, :]
    lane = lax.broadcasted_iota(jnp.int32, (slots, LANES), 1)
    table = jnp.where(lane == TILE, -1, 0)
    entry = jnp.where(lane[0:1, :] == TILE, lax.rem(items[...], 2) + 1, items[...])
    hit_int = jnp.where(hit, 1, 0)
    for i in range(used):
        table = table + hit_int[:, i:i + 1] * entry[i:i + 1, :]
    for d in range(row):
        send_table[d, 0:capacity, :] = table[d * capacity:(d + 1) * capacity, :]

    def table_copy(e, py, pz):
        return pltpu.make_async_remote_copy(
            src_ref=send_table.at[py * nz + pz], dst_ref=recv_table.at[e],
            send_sem=table_send.at[e], recv_sem=table_recv.at[e],
            device_id={"gy": py, "gz": pz}, device_id_type=MESH,
        )

    def brick_copy(e, py, pz):
        return pltpu.make_async_remote_copy(
            src_ref=send_buf.at[e], dst_ref=recv_buf.at[e],
            send_sem=brick_send.at[e], recv_sem=brick_recv.at[e],
            device_id={"gy": py, "gz": pz}, device_id_type=MESH,
        )

    def gather(source, chosen, py, pz, into, e):
        for c in range(capacity):
            into[e, c] = source[chosen[(py * nz + pz) * capacity + c]]

    pieces = ny if count % ny == 0 else 1
    depth = count // pieces

    def block_copy(way, d, j):
        part = pl.ds(j * depth, depth)
        return pltpu.make_async_remote_copy(
            src_ref=held(way, d).at[part], dst_ref=held(way, d + 1).at[part],
            send_sem=block_send.at[(way * nz + d) * pieces + j],
            recv_sem=block_recv.at[(way * nz + d + 1) * pieces + j],
            device_id={"gy": my_y, "gz": way_to[way]}, device_id_type=MESH,
        )

    def column_copy(dz, pz):
        return pltpu.make_async_remote_copy(
            src_ref=chosen_v, dst_ref=column_v.at[dz],
            send_sem=column_send.at[dz], recv_sem=column_recv.at[dz],
            device_id={"gy": my_y, "gz": pz}, device_id_type=MESH,
        )

    def far_copy(way, dy, py):
        place = step_of(way, nz - 1) * ny + dy
        return pltpu.make_async_remote_copy(
            src_ref=far_buf.at[way * ny + dy], dst_ref=recv_buf.at[place],
            send_sem=far_send.at[way * ny + dy], recv_sem=brick_recv.at[place],
            device_id={"gy": py, "gz": way_to[way]}, device_id_type=MESH,
        )

    def far(way):
        for dy in range(ny):
            py = lax.rem(my_y + dy, ny)
            chosen = column_s.at[step_of(way, nz - 2), 0]
            gather(held(way, nz - 2), chosen, py, way_to[way], far_buf, way * ny + dy)
            far_copy(way, dy, py).start()

    def offer(way, d, j):
        @pl.when(exists(way, d) & has_next[way])
        def _():
            block_copy(way, d, j).start()

    def share(block, chosen, dz, dy):
        py, pz = peer(dy, 0)
        gather(block, chosen, py, pz, send_buf, dz * ny + dy)
        brick_copy(dz * ny + dy, py, pz).start()

    load_bricks.wait()
    load_chosen.wait()
    pl.semaphore_wait(barrier, row - 1)
    for way in range(2):
        offer(way, 0, 0)
    for dz in range(1, nz):
        column_copy(dz, lax.rem(my_z + dz, nz)).start()
    for e in range(1, row):
        table_copy(e, *peer(e % ny, e // ny)).start()
    for j in range(1, max(ny, pieces)):
        if j < pieces:
            for way in range(2):
                offer(way, 0, j)
        if j < ny:
            share(bricks, chosen_s.at[0], 0, j)

    gather(bricks, chosen_s.at[0], my_y, my_z, recv_buf, 0)
    column_v[0] = chosen_v[...]
    recv_table[0] = send_table[my_y * nz + my_z]
    rows = lax.broadcasted_iota(jnp.int32, (extent, extent), 0)
    cols = lax.broadcasted_iota(jnp.int32, (extent, extent), 1)
    spacing[...] = (rows - cols).astype(F32)

    def table_arrived(e, _):
        table_copy(e, my_y, my_z).wait_recv()
        return 0

    lax.fori_loop(1, row, table_arrived, 0)
    for dz in range(1, nz):
        column_copy(dz, my_z).wait_recv()
    load_column = pltpu.make_async_copy(column_v, column_s, local_sem.at[4])
    load_column.start()
    keys[...] = jnp.full(keys.shape, -1, jnp.int32)
    for e in range(row):
        keys[e * capacity:(e + 1) * capacity, :] = recv_table[e, 0:capacity, :]
    view = keys[:, VIEW:VIEW + 1]
    for axis in range(2):
        slope = jnp.zeros((size, 1), F32)
        for v in range(views):
            slope = jnp.where(view == v, shear[v:v + 1, axis:axis + 1], slope)
        offset = keys[:, OFF_X + axis:OFF_X + axis + 1].astype(F32)
        for k in range(layers):
            shift_v[:, 3 * k + axis:3 * k + axis + 1] = offset + float(k - layers // 2) * slope
    strength = keys[:, ABSORB:ABSORB + 1].astype(F32) * (1.0 / ABSORB_UNIT)
    for k in range(layers):
        shift_v[:, 3 * k + 2:3 * k + 3] = jnp.where(keys[:, LIVE:LIVE + 1] > k, strength, 0.0)
    to_shift = pltpu.make_async_copy(shift_v, shift_s, local_sem.at[3])
    to_shift.start()
    tile = keys[:, TILE:TILE + 1]
    key = jnp.where(tile < 0, 2, tile) * (1 << 20) + keys[:, RANK:RANK + 1]
    key = jnp.broadcast_to(key, (size, size))
    other = key.T
    ahead = (other < key) | ((other == key) & (it < me))
    place = jnp.sum(jnp.where(ahead, 1, 0), axis=1, keepdims=True)
    hit = place == it
    sort_v[0:1, :] = jnp.sum(jnp.where(hit, me, 0), axis=0, keepdims=True)
    sort_v[1:2, :] = jnp.sum(jnp.where(hit & (tile == 0), 1, 0), axis=0, keepdims=True)
    sort_v[2:3, :] = jnp.sum(jnp.where(hit & (tile == 1), 1, 0), axis=0, keepdims=True)
    to_sort = pltpu.make_async_copy(sort_v, sort_s, local_sem.at[2])
    to_sort.start()
    to_shift.wait()
    to_sort.wait()
    load_column.wait()

    def interp(distance):
        return jnp.maximum(0.0, 1.0 - jnp.abs(distance)).astype(BF16)

    strip_rows = 32

    def render(e):
        spots = [e * capacity + c for c in range(capacity)]
        for c in range(capacity):
            for k in range(layers):
                across = interp(spacing[...] - shift_s[spots[c], 3 * k])
                downward_t = interp(spacing[...] + shift_s[spots[c], 3 * k + 1])
                halfway = jnp.dot(across, recv_buf[e, c, k], preferred_element_type=F32).astype(BF16)
                dense[c, k] = jnp.dot(halfway, downward_t, preferred_element_type=F32)
        for c in range(capacity):
            for begin in range(0, extent, strip_rows):
                lines = slice(begin, begin + strip_rows)
                optical, clear, colors = None, None, [None] * 3
                for k in range(layers):
                    density = dense[c, k, lines, :]
                    rate = shift_s[spots[c], 3 * k + 2]
                    soft = jnp.maximum(density, 0.0) + jnp.log(1.0 + jnp.exp(-jnp.abs(density)))
                    thickness = rate * soft
                    passed = jnp.exp(-thickness)
                    half_alpha = 0.5 - 0.5 * passed
                    if k:
                        half_alpha = half_alpha * clear
                    for n in range(3):
                        lit = half_alpha + half_alpha * jnp.tanh(
                            (0.5 * gain[n]) * density + 0.5 * bias[n]
                        )
                        colors[n] = lit if k == 0 else colors[n] + lit
                    optical = thickness if k == 0 else optical + thickness
                    clear = passed if k == 0 else clear * passed
                for n in range(3):
                    foot[spots[c], n, lines, :] = colors[n].astype(BF16)
                foot[spots[c], 3, lines, :] = optical.astype(BF16)

    for d in range(nz):
        below = exists(0, d)
        number = jnp.int32(1) if d == 0 else below.astype(jnp.int32) + exists(1, d).astype(jnp.int32)

        def entry(i, _):
            if d + 1 < whole:
                for way in range(2):
                    @pl.when(exists(way, d + 1) & (i < pieces))
                    def _():
                        block_copy(way, d, i).wait_recv()
                        if d + 2 < whole:
                            offer(way, d + 1, i)

                @pl.when(i == pieces - 1)
                def _():
                    for way in range(2):
                        if d + 2 == whole and whole < nz:
                            @pl.when(exists(way, d + 1) & has_next[way])
                            def _():
                                far(way)

                    for way in range(2):
                        @pl.when(exists(way, d + 1))
                        def _():
                            dz = step_of(way, d + 1)
                            for dy in range(1, ny):
                                share(held(way, d + 1), column_s.at[dz, 0], dz, dy)
                            gather(held(way, d + 1), column_s.at[dz, 0], my_y, my_z, recv_buf, dz * ny)

            dz = jnp.where((i < ny) & below, d, nz - d)
            e = dz * ny + lax.rem(i, ny)

            @pl.when((lax.rem(i, ny) > 0) | (d >= whole))
            def _():
                brick_copy(e, my_y, my_z).wait_recv()

            render(e)
            return 0

        lax.fori_loop(0, number * ny, entry, 0)

    def left(e, _):
        table_copy(e, my_y, my_z).wait_send()

        sent = lax.rem(e, ny) > 0
        if whole < nz:
            dz = lax.div(e, ny)
            first, last = (my_z == 0) & (dz == 1), (my_z == nz - 1) & (dz == nz - 1)
            sent = sent & jnp.logical_not(first | last)

        @pl.when(sent)
        def _():
            brick_copy(e, my_y, my_z).wait_send()

        return 0

    lax.fori_loop(1, row, left, 0)
    for dz in range(1, nz):
        column_copy(dz, my_z).wait_send()
    for way in range(2):
        for d in range(whole - 1):
            @pl.when(exists(way, d) & has_next[way])
            def _():
                for j in range(pieces):
                    block_copy(way, d, j).wait_send()
        if whole < nz:
            @pl.when(exists(way, whole - 1) & has_next[way])
            def _():
                for dy in range(ny):
                    far_copy(way, dy, my_y).wait_send()

    height = 16

    def strip(r, _):
        lines = pl.ds(pl.multiple_of(r * height, height), height)

        def visit(p, carry):
            optical0, optical1, color0, color1 = carry
            which = sort_s[0, p]
            in0 = sort_s[1, p].astype(F32)
            in1 = sort_s[2, p].astype(F32)
            clear = jnp.exp(-(optical0 * in0 + optical1 * in1))
            clear0, clear1 = clear * in0, clear * in1
            shade = [foot[which, n, lines, :].astype(F32) for n in range(3)]
            depth = foot[which, 3, lines, :].astype(F32)
            return (
                optical0 + in0 * depth,
                optical1 + in1 * depth,
                tuple(c + clear0 * s for c, s in zip(color0, shade)),
                tuple(c + clear1 * s for c, s in zip(color1, shade)),
            )

        zero = jnp.zeros((height, extent), F32)
        optical0, optical1, color0, color1 = lax.fori_loop(
            0, slots, visit, (zero, zero, (zero,) * 3, (zero,) * 3), unroll=4
        )
        for n in range(3):
            out[0, n, lines, :] = color0[n]
            out[1, n, lines, :] = color1[n]
        out[0, 3, lines, :] = jnp.exp(-optical0)
        out[1, 3, lines, :] = jnp.exp(-optical1)
        return 0

    lax.fori_loop(0, extent // height, strip, 0)


def body(ny, nz, bricks, live, shear, offsets, absorb, color_gain, color_bias, targets, order):
    brick_count, layers, extent, _ = bricks.shape
    views = shear.shape[0]
    row = ny * nz
    capacity = (brick_count * views + row - 1) // row
    slots = row * capacity
    smem = pl.BlockSpec(memory_space=pltpu.SMEM)
    vmem = pl.BlockSpec(memory_space=pltpu.VMEM)
    hbm = pl.BlockSpec(memory_space=pltpu.HBM)
    live_row, absorb_row = live.reshape(1, brick_count), absorb.reshape(1, brick_count)
    table_rows = (capacity + 7) // 8 * 8
    longest = max(slots, brick_count * views)
    size = (longest + LANES - 1) // LANES * LANES
    return pl.pallas_call(
        functools.partial(main_kernel, ny, nz, capacity),
        out_shape=jax.ShapeDtypeStruct((2, 4, extent, extent), F32),
        in_specs=[hbm, hbm, hbm, hbm, hbm, smem, smem, hbm, hbm],
        out_specs=vmem,
        scratch_shapes=[
            pltpu.VMEM(bricks.shape, BF16),
            pltpu.VMEM((nz, 8, size), jnp.int32),
            pltpu.SMEM((nz, 8, size), jnp.int32),
            pltpu.VMEM((row, capacity, layers, extent, extent), BF16),
            pltpu.VMEM((row, capacity, layers, extent, extent), BF16),
            pltpu.VMEM((row, table_rows, LANES), jnp.int32),
            pltpu.VMEM((row, table_rows, LANES), jnp.int32),
            pltpu.VMEM((LANES, LANES), jnp.int32),
            pltpu.VMEM((size, LANES), jnp.int32),
            pltpu.VMEM((8, size), jnp.int32),
            pltpu.SMEM((8, size), jnp.int32),
            pltpu.VMEM((size, LANES), F32),
            pltpu.SMEM((size, LANES), F32),
            pltpu.VMEM((8, size), jnp.int32),
            pltpu.SMEM((8, size), jnp.int32),
            pltpu.VMEM((extent, extent), F32),
            pltpu.VMEM((capacity, layers, extent, extent), F32),
            pltpu.VMEM((slots, 4, extent, extent), BF16),
            pltpu.VMEM((size, LANES), jnp.int32),
            pltpu.SemaphoreType.DMA((row,)),
            pltpu.SemaphoreType.DMA((row,)),
            pltpu.SemaphoreType.DMA((row,)),
            pltpu.SemaphoreType.DMA((row,)),
            pltpu.SemaphoreType.DMA((nz,)),
            pltpu.SemaphoreType.DMA((nz,)),
            pltpu.SemaphoreType.DMA((2 * nz * ny,)),
            pltpu.SemaphoreType.DMA((2 * nz * ny,)),
            pltpu.VMEM((2 * ny, capacity, layers, extent, extent), BF16),
            pltpu.SemaphoreType.DMA((2 * ny,)),
            pltpu.SemaphoreType.DMA((11,)),
            *[
                pltpu.VMEM(a.shape, a.dtype)
                for a in (live_row, shear, offsets, absorb_row, targets, order)
            ],
            *[pltpu.VMEM(bricks.shape, BF16) for _ in range(2 * (nz - 1))],
        ],
        compiler_params=pltpu.CompilerParams(
            collective_id=0, has_side_effects=True, vmem_limit_bytes=48 * 1024 * 1024
        ),
    )(
        bricks, live_row, shear, offsets, absorb_row,
        color_gain, color_bias, targets, order,
    )


def solution(mesh):
    ny, nz = mesh.shape["gy"], mesh.shape["gz"]
    split = ("gx", "gy", "gz")
    placed = (
        P(split, None, None, None),
        P(split),
        P(),
        P(split, None, None),
        P(split),
        P(),
        P(),
        P(split, None),
        P(None, split),
    )
    return jax.shard_map(
        functools.partial(body, ny, nz),
        mesh=mesh,
        in_specs=placed,
        out_specs=P(split, None, None, None),
        check_vma=False,
    )
```

```python
import functools

import jax
import jax.numpy as jnp
from jax import lax
from jax.experimental import pallas as pl
from jax.experimental.pallas import tpu as pltpu
from jax.sharding import PartitionSpec as P

MESH = pl.DeviceIdType.MESH
F32 = jnp.float32
BF16 = jnp.bfloat16
LANES = 128
ABSORB_UNIT = float(2**20)
OFF_X, OFF_Y, LIVE, VIEW, ABSORB, TILE, RANK, BRICK = range(8)


def main_kernel(
    ny, nz, capacity,
    bricks_in, live_in, shear_in, offsets_in, absorb_in, gain, bias, targets_in, order_in,
    out,
    bricks, column_v, column_s, send_buf, recv_buf, send_table, recv_table, raw, items, chosen_v, chosen_s,
    shift_v, shift_s, sort_v, sort_s, spacing, dense, foot, keys,
    table_send, table_recv, brick_send, brick_recv, column_send, column_recv, block_send, block_recv,
    far_buf, far_send, local_sem, live, shear, offsets, absorb, targets, order, *blocks,
):
    row = ny * nz
    slots = row * capacity
    count, layers, extent, _ = bricks_in.shape
    views = targets_in.shape[0]
    size = keys.shape[0]
    my_y, my_z = lax.axis_index("gy"), lax.axis_index("gz")
    way_to = (my_z + 1, my_z - 1)
    has_next = (my_z + 1 < nz, my_z >= 1)

    def exists(way, d):
        return my_z >= d if way == 0 else my_z + d < nz

    def step_of(way, d):
        return d if way == 0 else nz - d

    whole = nz - 1 if nz >= 3 else nz

    def held(way, d):
        return blocks[way * (nz - 1) + d - 1] if d else bricks

    def peer(dy, dz):
        return lax.rem(my_y + dy, ny), lax.rem(my_z + dz, nz)

    barrier = pltpu.get_barrier_semaphore()
    for e in range(1, row):
        py, pz = peer(e % ny, e // ny)
        pl.semaphore_signal(barrier, inc=1, device_id={"gy": py, "gz": pz}, device_id_type=MESH)

    load_bricks = pltpu.make_async_copy(bricks_in, bricks, local_sem.at[0])
    loads = [
        pltpu.make_async_copy(source, into, local_sem.at[5 + n])
        for n, (source, into) in enumerate((
            (live_in, live), (shear_in, shear), (offsets_in, offsets),
            (absorb_in, absorb), (targets_in, targets), (order_in, order),
        ))
    ]
    for load in loads:
        load.start()
    load_bricks.start()
    for load in loads:
        load.wait()

    raw[...] = jnp.zeros(raw.shape, jnp.int32)
    raw[0:views, 0:count] = order[...]
    raw[views:2 * views, 0:count] = targets[...]
    for v in range(views):
        raw[2 * views + 2 * v:2 * views + 2 * v + 2, 0:count] = offsets[v]
    raw[4 * views:4 * views + 1, 0:count] = live[...]
    units = jnp.round(absorb[...].astype(F32) * ABSORB_UNIT)
    raw[4 * views + 1:4 * views + 2, 0:count] = units.astype(jnp.int32)
    turned = raw[...].T
    items[...] = jnp.zeros(items.shape, jnp.int32)
    for v in range(views):
        mine = slice(v * count, (v + 1) * count)
        at = 2 * views + 2 * v
        items[mine, OFF_X:OFF_Y + 1] = turned[0:count, at:at + 2]
        items[mine, LIVE:LIVE + 1] = turned[0:count, 4 * views:4 * views + 1]
        items[mine, VIEW:VIEW + 1] = jnp.full((count, 1), v, jnp.int32)
        items[mine, ABSORB:ABSORB + 1] = turned[0:count, 4 * views + 1:4 * views + 2]
        items[mine, TILE:TILE + 1] = turned[0:count, views + v:views + v + 1]
        items[mine, RANK:RANK + 1] = turned[0:count, v:v + 1]
        items[mine, BRICK:BRICK + 1] = lax.broadcasted_iota(jnp.int32, (count, 1), 0)
    me = lax.broadcasted_iota(jnp.int32, (size, size), 0)
    it = lax.broadcasted_iota(jnp.int32, (size, size), 1)
    used = views * count
    owner = jnp.where(me < used, lax.rem(lax.div(items[:, TILE:TILE + 1], 2), row), -1)
    same = (owner == owner.T) & (it < me)
    slot = owner * capacity + jnp.sum(jnp.where(same, 1, 0), axis=1, keepdims=True)
    slot = jnp.where(me < used, slot, -1)
    chosen_v[0:1, :] = jnp.sum(
        jnp.where(slot == it, items[:, BRICK:BRICK + 1], 0), axis=0, keepdims=True
    )
    load_chosen = pltpu.make_async_copy(chosen_v, chosen_s, local_sem.at[1])
    load_chosen.start()
    hit = (slot.T == me)[0:slots, :]
    lane = lax.broadcasted_iota(jnp.int32, (slots, LANES), 1)
    table = jnp.where(lane == TILE, -1, 0)
    entry = jnp.where(lane[0:1, :] == TILE, lax.rem(items[...], 2) + 1, items[...])
    hit_int = jnp.where(hit, 1, 0)
    for i in range(used):
        table = table + hit_int[:, i:i + 1] * entry[i:i + 1, :]
    for d in range(row):
        send_table[d, 0:capacity, :] = table[d * capacity:(d + 1) * capacity, :]

    def table_copy(e, py, pz):
        return pltpu.make_async_remote_copy(
            src_ref=send_table.at[py * nz + pz], dst_ref=recv_table.at[e],
            send_sem=table_send.at[e], recv_sem=table_recv.at[e],
            device_id={"gy": py, "gz": pz}, device_id_type=MESH,
        )

    def brick_copy(e, py, pz):
        return pltpu.make_async_remote_copy(
            src_ref=send_buf.at[e], dst_ref=recv_buf.at[e],
            send_sem=brick_send.at[e], recv_sem=brick_recv.at[e],
            device_id={"gy": py, "gz": pz}, device_id_type=MESH,
        )

    def gather(source, chosen, py, pz, into, e):
        for c in range(capacity):
            into[e, c] = source[chosen[(py * nz + pz) * capacity + c]]

    pieces = ny if count % ny == 0 else 1
    depth = count // pieces

    def block_copy(way, d, j):
        part = pl.ds(j * depth, depth)
        return pltpu.make_async_remote_copy(
            src_ref=held(way, d).at[part], dst_ref=held(way, d + 1).at[part],
            send_sem=block_send.at[(way * nz + d) * pieces + j],
            recv_sem=block_recv.at[(way * nz + d + 1) * pieces + j],
            device_id={"gy": my_y, "gz": way_to[way]}, device_id_type=MESH,
        )

    def column_copy(dz, pz):
        return pltpu.make_async_remote_copy(
            src_ref=chosen_v, dst_ref=column_v.at[dz],
            send_sem=column_send.at[dz], recv_sem=column_recv.at[dz],
            device_id={"gy": my_y, "gz": pz}, device_id_type=MESH,
        )

    def far_copy(way, dy, py):
        place = step_of(way, nz - 1) * ny + dy
        return pltpu.make_async_remote_copy(
            src_ref=far_buf.at[way * ny + dy], dst_ref=recv_buf.at[place],
            send_sem=far_send.at[way * ny + dy], recv_sem=brick_recv.at[place],
            device_id={"gy": py, "gz": way_to[way]}, device_id_type=MESH,
        )

    def far(way):
        for dy in range(ny):
            py = lax.rem(my_y + dy, ny)
            chosen = column_s.at[step_of(way, nz - 2), 0]
            gather(held(way, nz - 2), chosen, py, way_to[way], far_buf, way * ny + dy)
            far_copy(way, dy, py).start()

    def offer(way, d, j):
        @pl.when(exists(way, d) & has_next[way])
        def _():
            block_copy(way, d, j).start()

    def share(block, chosen, dz, dy):
        py, pz = peer(dy, 0)
        gather(block, chosen, py, pz, send_buf, dz * ny + dy)
        brick_copy(dz * ny + dy, py, pz).start()

    load_bricks.wait()
    load_chosen.wait()
    pl.semaphore_wait(barrier, row - 1)
    for way in range(2):
        offer(way, 0, 0)
    for dz in range(1, nz):
        column_copy(dz, lax.rem(my_z + dz, nz)).start()
    for e in range(1, row):
        table_copy(e, *peer(e % ny, e // ny)).start()
    for j in range(1, max(ny, pieces)):
        if j < pieces:
            for way in range(2):
                offer(way, 0, j)
        if j < ny:
            share(bricks, chosen_s.at[0], 0, j)

    gather(bricks, chosen_s.at[0], my_y, my_z, recv_buf, 0)
    column_v[0] = chosen_v[...]
    recv_table[0] = send_table[my_y * nz + my_z]
    rows = lax.broadcasted_iota(jnp.int32, (extent, extent), 0)
    cols = lax.broadcasted_iota(jnp.int32, (extent, extent), 1)
    spacing[...] = (rows - cols).astype(F32)

    def table_arrived(e, _):
        table_copy(e, my_y, my_z).wait_recv()
        return 0

    lax.fori_loop(1, row, table_arrived, 0)
    for dz in range(1, nz):
        column_copy(dz, my_z).wait_recv()
    load_column = pltpu.make_async_copy(column_v, column_s, local_sem.at[4])
    load_column.start()
    keys[...] = jnp.full(keys.shape, -1, jnp.int32)
    for e in range(row):
        keys[e * capacity:(e + 1) * capacity, :] = recv_table[e, 0:capacity, :]
    view = keys[:, VIEW:VIEW + 1]
    for axis in range(2):
        slope = jnp.zeros((size, 1), F32)
        for v in range(views):
            slope = jnp.where(view == v, shear[axis:axis + 1, v:v + 1], slope)
        offset = keys[:, OFF_X + axis:OFF_X + axis + 1].astype(F32)
        for k in range(layers):
            shift_v[:, 3 * k + axis:3 * k + axis + 1] = offset + float(k - layers // 2) * slope
    strength = keys[:, ABSORB:ABSORB + 1].astype(F32) * (1.0 / ABSORB_UNIT)
    for k in range(layers):
        shift_v[:, 3 * k + 2:3 * k + 3] = jnp.where(keys[:, LIVE:LIVE + 1] > k, strength, 0.0)
    to_shift = pltpu.make_async_copy(shift_v, shift_s, local_sem.at[3])
    to_shift.start()
    tile = keys[:, TILE:TILE + 1]
    key = jnp.where(tile < 0, 2, tile) * (1 << 20) + keys[:, RANK:RANK + 1]
    key = jnp.broadcast_to(key, (size, size))
    other = key.T
    ahead = (other < key) | ((other == key) & (it < me))
    place = jnp.sum(jnp.where(ahead, 1, 0), axis=1, keepdims=True)
    hit = place == it
    sort_v[0:1, :] = jnp.sum(jnp.where(hit, me, 0), axis=0, keepdims=True)
    sort_v[1:2, :] = jnp.sum(jnp.where(hit & (tile == 0), 1, 0), axis=0, keepdims=True)
    sort_v[2:3, :] = jnp.sum(jnp.where(hit & (tile == 1), 1, 0), axis=0, keepdims=True)
    to_sort = pltpu.make_async_copy(sort_v, sort_s, local_sem.at[2])
    to_sort.start()
    to_shift.wait()
    to_sort.wait()
    load_column.wait()

    def interp(distance):
        return jnp.maximum(0.0, 1.0 - jnp.abs(distance)).astype(BF16)

    strip_rows = 32

    def render(e):
        spots = [e * capacity + c for c in range(capacity)]
        for c in range(capacity):
            for k in range(layers):
                across = interp(spacing[...] - shift_s[spots[c], 3 * k])
                downward_t = interp(spacing[...] + shift_s[spots[c], 3 * k + 1])
                halfway = jnp.dot(across, recv_buf[e, c, k], preferred_element_type=F32).astype(BF16)
                dense[c, k] = jnp.dot(halfway, downward_t, preferred_element_type=F32)
        for c in range(capacity):
            for begin in range(0, extent, strip_rows):
                lines = slice(begin, begin + strip_rows)
                optical, clear, colors = None, None, [None] * 3
                for k in range(layers):
                    density = dense[c, k, lines, :]
                    rate = shift_s[spots[c], 3 * k + 2]
                    soft = jnp.maximum(density, 0.0) + jnp.log(1.0 + jnp.exp(-jnp.abs(density)))
                    thickness = rate * soft
                    passed = jnp.exp(-thickness)
                    half_alpha = 0.5 - 0.5 * passed
                    if k:
                        half_alpha = half_alpha * clear
                    for n in range(3):
                        lit = half_alpha + half_alpha * jnp.tanh(
                            (0.5 * gain[n]) * density + 0.5 * bias[n]
                        )
                        colors[n] = lit if k == 0 else colors[n] + lit
                    optical = thickness if k == 0 else optical + thickness
                    clear = passed if k == 0 else clear * passed
                for n in range(3):
                    foot[spots[c], n, lines, :] = colors[n].astype(BF16)
                foot[spots[c], 3, lines, :] = optical.astype(BF16)

    for d in range(nz):
        below = exists(0, d)
        number = jnp.int32(1) if d == 0 else below.astype(jnp.int32) + exists(1, d).astype(jnp.int32)

        def entry(i, _):
            if d + 1 < whole:
                for way in range(2):
                    @pl.when(exists(way, d + 1) & (i < pieces))
                    def _():
                        block_copy(way, d, i).wait_recv()
                        if d + 2 < whole:
                            offer(way, d + 1, i)

                @pl.when(i == pieces - 1)
                def _():
                    for way in range(2):
                        if d + 2 == whole and whole < nz:
                            @pl.when(exists(way, d + 1) & has_next[way])
                            def _():
                                far(way)

                    for way in range(2):
                        @pl.when(exists(way, d + 1))
                        def _():
                            dz = step_of(way, d + 1)
                            for dy in range(1, ny):
                                share(held(way, d + 1), column_s.at[dz, 0], dz, dy)
                            gather(held(way, d + 1), column_s.at[dz, 0], my_y, my_z, recv_buf, dz * ny)

            dz = jnp.where((i < ny) & below, d, nz - d)
            e = dz * ny + lax.rem(i, ny)

            @pl.when((lax.rem(i, ny) > 0) | (d >= whole))
            def _():
                brick_copy(e, my_y, my_z).wait_recv()

            render(e)
            return 0

        lax.fori_loop(0, number * ny, entry, 0)

    def left(e, _):
        table_copy(e, my_y, my_z).wait_send()

        sent = lax.rem(e, ny) > 0
        if whole < nz:
            dz = lax.div(e, ny)
            first, last = (my_z == 0) & (dz == 1), (my_z == nz - 1) & (dz == nz - 1)
            sent = sent & jnp.logical_not(first | last)

        @pl.when(sent)
        def _():
            brick_copy(e, my_y, my_z).wait_send()

        return 0

    lax.fori_loop(1, row, left, 0)
    for dz in range(1, nz):
        column_copy(dz, my_z).wait_send()
    for way in range(2):
        for d in range(whole - 1):
            @pl.when(exists(way, d) & has_next[way])
            def _():
                for j in range(pieces):
                    block_copy(way, d, j).wait_send()
        if whole < nz:
            @pl.when(exists(way, whole - 1) & has_next[way])
            def _():
                for dy in range(ny):
                    far_copy(way, dy, my_y).wait_send()

    height = 16

    def strip(r, _):
        lines = pl.ds(pl.multiple_of(r * height, height), height)

        def visit(p, carry):
            optical0, optical1, color0, color1 = carry
            which = sort_s[0, p]
            in0 = sort_s[1, p].astype(F32)
            in1 = sort_s[2, p].astype(F32)
            clear = jnp.exp(-(optical0 * in0 + optical1 * in1))
            clear0, clear1 = clear * in0, clear * in1
            shade = [foot[which, n, lines, :].astype(F32) for n in range(3)]
            depth = foot[which, 3, lines, :].astype(F32)
            return (
                optical0 + in0 * depth,
                optical1 + in1 * depth,
                tuple(c + clear0 * s for c, s in zip(color0, shade)),
                tuple(c + clear1 * s for c, s in zip(color1, shade)),
            )

        zero = jnp.zeros((height, extent), F32)
        optical0, optical1, color0, color1 = lax.fori_loop(
            0, slots, visit, (zero, zero, (zero,) * 3, (zero,) * 3), unroll=4
        )
        for n in range(3):
            out[0, n, lines, :] = color0[n]
            out[1, n, lines, :] = color1[n]
        out[0, 3, lines, :] = jnp.exp(-optical0)
        out[1, 3, lines, :] = jnp.exp(-optical1)
        return 0

    lax.fori_loop(0, extent // height, strip, 0)


def body(ny, nz, bricks, live, shear, offsets, absorb, color_gain, color_bias, targets, order):
    brick_count, layers, extent, _ = bricks.shape
    views = targets.shape[1]
    row = ny * nz
    capacity = (brick_count * views + row - 1) // row
    slots = row * capacity
    smem = pl.BlockSpec(memory_space=pltpu.SMEM)
    vmem = pl.BlockSpec(memory_space=pltpu.VMEM)
    hbm = pl.BlockSpec(memory_space=pltpu.HBM)
    shear, offsets, targets = shear.T, offsets.transpose(1, 2, 0), targets.T
    live_row, absorb_row = live.reshape(1, brick_count), absorb.reshape(1, brick_count)
    table_rows = (capacity + 7) // 8 * 8
    longest = max(slots, brick_count * views)
    size = (longest + LANES - 1) // LANES * LANES
    return pl.pallas_call(
        functools.partial(main_kernel, ny, nz, capacity),
        out_shape=jax.ShapeDtypeStruct((2, 4, extent, extent), F32),
        in_specs=[hbm, hbm, hbm, hbm, hbm, smem, smem, hbm, hbm],
        out_specs=vmem,
        scratch_shapes=[
            pltpu.VMEM(bricks.shape, BF16),
            pltpu.VMEM((nz, 8, size), jnp.int32),
            pltpu.SMEM((nz, 8, size), jnp.int32),
            pltpu.VMEM((row, capacity, layers, extent, extent), BF16),
            pltpu.VMEM((row, capacity, layers, extent, extent), BF16),
            pltpu.VMEM((row, table_rows, LANES), jnp.int32),
            pltpu.VMEM((row, table_rows, LANES), jnp.int32),
            pltpu.VMEM((LANES, LANES), jnp.int32),
            pltpu.VMEM((size, LANES), jnp.int32),
            pltpu.VMEM((8, size), jnp.int32),
            pltpu.SMEM((8, size), jnp.int32),
            pltpu.VMEM((size, LANES), F32),
            pltpu.SMEM((size, LANES), F32),
            pltpu.VMEM((8, size), jnp.int32),
            pltpu.SMEM((8, size), jnp.int32),
            pltpu.VMEM((extent, extent), F32),
            pltpu.VMEM((capacity, layers, extent, extent), F32),
            pltpu.VMEM((slots, 4, extent, extent), BF16),
            pltpu.VMEM((size, LANES), jnp.int32),
            pltpu.SemaphoreType.DMA((row,)),
            pltpu.SemaphoreType.DMA((row,)),
            pltpu.SemaphoreType.DMA((row,)),
            pltpu.SemaphoreType.DMA((row,)),
            pltpu.SemaphoreType.DMA((nz,)),
            pltpu.SemaphoreType.DMA((nz,)),
            pltpu.SemaphoreType.DMA((2 * nz * ny,)),
            pltpu.SemaphoreType.DMA((2 * nz * ny,)),
            pltpu.VMEM((2 * ny, capacity, layers, extent, extent), BF16),
            pltpu.SemaphoreType.DMA((2 * ny,)),
            pltpu.SemaphoreType.DMA((11,)),
            *[
                pltpu.VMEM(a.shape, a.dtype)
                for a in (live_row, shear, offsets, absorb_row, targets, order)
            ],
            *[pltpu.VMEM(bricks.shape, BF16) for _ in range(2 * (nz - 1))],
        ],
        compiler_params=pltpu.CompilerParams(
            collective_id=0, has_side_effects=True, vmem_limit_bytes=60 * 1024 * 1024
        ),
    )(
        bricks, live_row, shear, offsets, absorb_row,
        color_gain, color_bias, targets, order,
    )


def solution(mesh):
    ny, nz = mesh.shape["gy"], mesh.shape["gz"]
    split = ("gx", "gy", "gz")
    placed = (
        P(split, None, None, None),
        P(split),
        P(),
        P(split, None, None),
        P(split),
        P(),
        P(),
        P(split, None),
        P(None, split),
    )
    return jax.shard_map(
        functools.partial(body, ny, nz),
        mesh=mesh,
        in_specs=placed,
        out_specs=P(split, None, None, None),
        check_vma=False,
    )
```

```python
import functools

import jax
import jax.numpy as jnp
from jax import lax
from jax.experimental import pallas as pl
from jax.experimental.pallas import tpu as pltpu
from jax.sharding import PartitionSpec as P

MESH = pl.DeviceIdType.MESH
F32 = jnp.float32
BF16 = jnp.bfloat16
LANES = 128
ABSORB_UNIT = float(2**20)
OFF_X, OFF_Y, LIVE, VIEW, ABSORB, TILE, RANK, BRICK = range(8)


def main_kernel(
    ny, nz, capacity,
    bricks_in, live_in, shear_in, offsets_in, absorb_in, gain, bias, targets_in, order_in,
    out,
    bricks, column_v, column_s, send_buf, recv_buf, send_table, recv_table, raw, items, chosen_v, chosen_s,
    shift_v, shift_s, sort_v, sort_s, spacing, dense, foot, keys,
    table_send, table_recv, brick_send, brick_recv, column_send, column_recv, block_send, block_recv,
    far_buf, far_send, local_sem, live, shear, offsets, absorb, targets, order, *blocks,
):
    row = ny * nz
    slots = row * capacity
    count, layers, extent, _ = bricks_in.shape
    views = targets_in.shape[0]
    size = keys.shape[0]
    my_y, my_z = lax.axis_index("gy"), lax.axis_index("gz")
    way_to = (my_z + 1, my_z - 1)
    has_next = (my_z + 1 < nz, my_z >= 1)

    def exists(way, d):
        return my_z >= d if way == 0 else my_z + d < nz

    def step_of(way, d):
        return d if way == 0 else nz - d

    whole = nz - 1 if nz >= 3 else nz

    def held(way, d):
        return blocks[way * (nz - 1) + d - 1] if d else bricks

    def peer(dy, dz):
        return lax.rem(my_y + dy, ny), lax.rem(my_z + dz, nz)

    barrier = pltpu.get_barrier_semaphore()
    for e in range(1, row):
        py, pz = peer(e % ny, e // ny)
        pl.semaphore_signal(barrier, inc=1, device_id={"gy": py, "gz": pz}, device_id_type=MESH)

    load_bricks = pltpu.make_async_copy(bricks_in, bricks, local_sem.at[0])
    loads = [
        pltpu.make_async_copy(source, into, local_sem.at[5 + n])
        for n, (source, into) in enumerate((
            (live_in, live), (shear_in, shear), (offsets_in, offsets),
            (absorb_in, absorb), (targets_in, targets), (order_in, order),
        ))
    ]
    for load in loads:
        load.start()
    load_bricks.start()
    for load in loads:
        load.wait()

    raw[...] = jnp.zeros(raw.shape, jnp.int32)
    raw[0:views, 0:count] = order[...]
    raw[views:2 * views, 0:count] = targets[...]
    for v in range(views):
        raw[2 * views + 2 * v:2 * views + 2 * v + 2, 0:count] = offsets[v]
    raw[4 * views:4 * views + 1, 0:count] = live[...]
    units = jnp.round(absorb[...].astype(F32) * ABSORB_UNIT)
    raw[4 * views + 1:4 * views + 2, 0:count] = units.astype(jnp.int32)
    turned = raw[...].T
    items[...] = jnp.zeros(items.shape, jnp.int32)
    for v in range(views):
        mine = slice(v * count, (v + 1) * count)
        at = 2 * views + 2 * v
        items[mine, OFF_X:OFF_Y + 1] = turned[0:count, at:at + 2]
        items[mine, LIVE:LIVE + 1] = turned[0:count, 4 * views:4 * views + 1]
        items[mine, VIEW:VIEW + 1] = jnp.full((count, 1), v, jnp.int32)
        items[mine, ABSORB:ABSORB + 1] = turned[0:count, 4 * views + 1:4 * views + 2]
        items[mine, TILE:TILE + 1] = turned[0:count, views + v:views + v + 1]
        items[mine, RANK:RANK + 1] = turned[0:count, v:v + 1]
        items[mine, BRICK:BRICK + 1] = lax.broadcasted_iota(jnp.int32, (count, 1), 0)
    me = lax.broadcasted_iota(jnp.int32, (size, size), 0)
    it = lax.broadcasted_iota(jnp.int32, (size, size), 1)
    used = views * count
    owner = jnp.where(me < used, lax.rem(lax.div(items[:, TILE:TILE + 1], 2), row), -1)
    same = (owner == owner.T) & (it < me)
    slot = owner * capacity + jnp.sum(jnp.where(same, 1, 0), axis=1, keepdims=True)
    slot = jnp.where(me < used, slot, -1)
    chosen_v[0:1, :] = jnp.sum(
        jnp.where(slot == it, items[:, BRICK:BRICK + 1], 0), axis=0, keepdims=True
    )
    load_chosen = pltpu.make_async_copy(chosen_v, chosen_s, local_sem.at[1])
    load_chosen.start()
    hit = (slot.T == me)[0:slots, :]
    lane = lax.broadcasted_iota(jnp.int32, (slots, LANES), 1)
    table = jnp.where(lane == TILE, -1, 0)
    entry = jnp.where(lane[0:1, :] == TILE, lax.rem(items[...], 2) + 1, items[...])
    hit_int = jnp.where(hit, 1, 0)
    for i in range(used):
        table = table + hit_int[:, i:i + 1] * entry[i:i + 1, :]
    for d in range(row):
        send_table[d, 0:capacity, :] = table[d * capacity:(d + 1) * capacity, :]

    def table_copy(e, py, pz):
        return pltpu.make_async_remote_copy(
            src_ref=send_table.at[py * nz + pz], dst_ref=recv_table.at[e],
            send_sem=table_send.at[e], recv_sem=table_recv.at[e],
            device_id={"gy": py, "gz": pz}, device_id_type=MESH,
        )

    def brick_copy(e, py, pz):
        return pltpu.make_async_remote_copy(
            src_ref=send_buf.at[e], dst_ref=recv_buf.at[e],
            send_sem=brick_send.at[e], recv_sem=brick_recv.at[e],
            device_id={"gy": py, "gz": pz}, device_id_type=MESH,
        )

    def gather(source, chosen, py, pz, into, e):
        for c in range(capacity):
            into[e, c] = source[chosen[(py * nz + pz) * capacity + c]]

    pieces = ny if count % ny == 0 else 1
    depth = count // pieces

    def block_copy(way, d, j):
        part = pl.ds(j * depth, depth)
        return pltpu.make_async_remote_copy(
            src_ref=held(way, d).at[part], dst_ref=held(way, d + 1).at[part],
            send_sem=block_send.at[(way * nz + d) * pieces + j],
            recv_sem=block_recv.at[(way * nz + d + 1) * pieces + j],
            device_id={"gy": my_y, "gz": way_to[way]}, device_id_type=MESH,
        )

    def column_copy(dz, pz):
        return pltpu.make_async_remote_copy(
            src_ref=chosen_v, dst_ref=column_v.at[dz],
            send_sem=column_send.at[dz], recv_sem=column_recv.at[dz],
            device_id={"gy": my_y, "gz": pz}, device_id_type=MESH,
        )

    def far_copy(way, dy, py):
        place = step_of(way, nz - 1) * ny + dy
        return pltpu.make_async_remote_copy(
            src_ref=far_buf.at[way * ny + dy], dst_ref=recv_buf.at[place],
            send_sem=far_send.at[way * ny + dy], recv_sem=brick_recv.at[place],
            device_id={"gy": py, "gz": way_to[way]}, device_id_type=MESH,
        )

    def far(way):
        for dy in range(ny):
            py = lax.rem(my_y + dy, ny)
            chosen = column_s.at[step_of(way, nz - 2), 0]
            gather(held(way, nz - 2), chosen, py, way_to[way], far_buf, way * ny + dy)
            far_copy(way, dy, py).start()

    def offer(way, d, j):
        @pl.when(exists(way, d) & has_next[way])
        def _():
            block_copy(way, d, j).start()

    def share(block, chosen, dz, dy):
        py, pz = peer(dy, 0)
        gather(block, chosen, py, pz, send_buf, dz * ny + dy)
        brick_copy(dz * ny + dy, py, pz).start()

    load_bricks.wait()
    load_chosen.wait()
    pl.semaphore_wait(barrier, row - 1)
    for way in range(2):
        offer(way, 0, 0)
    for dz in range(1, nz):
        column_copy(dz, lax.rem(my_z + dz, nz)).start()
    for e in range(1, row):
        table_copy(e, *peer(e % ny, e // ny)).start()
    for j in range(1, max(ny, pieces)):
        if j < pieces:
            for way in range(2):
                offer(way, 0, j)
        if j < ny:
            share(bricks, chosen_s.at[0], 0, j)

    gather(bricks, chosen_s.at[0], my_y, my_z, recv_buf, 0)
    column_v[0] = chosen_v[...]
    recv_table[0] = send_table[my_y * nz + my_z]
    rows = lax.broadcasted_iota(jnp.int32, (extent, extent), 0)
    cols = lax.broadcasted_iota(jnp.int32, (extent, extent), 1)
    spacing[...] = (rows - cols).astype(F32)

    def table_arrived(e, _):
        table_copy(e, my_y, my_z).wait_recv()
        return 0

    lax.fori_loop(1, row, table_arrived, 0)
    for dz in range(1, nz):
        column_copy(dz, my_z).wait_recv()
    load_column = pltpu.make_async_copy(column_v, column_s, local_sem.at[4])
    load_column.start()
    keys[...] = jnp.full(keys.shape, -1, jnp.int32)
    for e in range(row):
        keys[e * capacity:(e + 1) * capacity, :] = recv_table[e, 0:capacity, :]
    view = keys[:, VIEW:VIEW + 1]
    for axis in range(2):
        slope = jnp.zeros((size, 1), F32)
        for v in range(views):
            slope = jnp.where(view == v, shear[axis:axis + 1, v:v + 1], slope)
        offset = keys[:, OFF_X + axis:OFF_X + axis + 1].astype(F32)
        for k in range(layers):
            shift_v[:, 3 * k + axis:3 * k + axis + 1] = offset + float(k - layers // 2) * slope
    strength = keys[:, ABSORB:ABSORB + 1].astype(F32) * (1.0 / ABSORB_UNIT)
    for k in range(layers):
        shift_v[:, 3 * k + 2:3 * k + 3] = jnp.where(keys[:, LIVE:LIVE + 1] > k, strength, 0.0)
    to_shift = pltpu.make_async_copy(shift_v, shift_s, local_sem.at[3])
    to_shift.start()
    tile = keys[:, TILE:TILE + 1]
    key = jnp.where(tile < 0, 2, tile) * (1 << 20) + keys[:, RANK:RANK + 1]
    key = jnp.broadcast_to(key, (size, size))
    other = key.T
    ahead = (other < key) | ((other == key) & (it < me))
    place = jnp.sum(jnp.where(ahead, 1, 0), axis=1, keepdims=True)
    hit = place == it
    sort_v[0:1, :] = jnp.sum(jnp.where(hit, me, 0), axis=0, keepdims=True)
    sort_v[1:2, :] = jnp.sum(jnp.where(hit & (tile == 0), 1, 0), axis=0, keepdims=True)
    sort_v[2:3, :] = jnp.sum(jnp.where(hit & (tile == 1), 1, 0), axis=0, keepdims=True)
    to_sort = pltpu.make_async_copy(sort_v, sort_s, local_sem.at[2])
    to_sort.start()
    to_shift.wait()
    to_sort.wait()
    load_column.wait()

    def interp(distance):
        return jnp.maximum(0.0, 1.0 - jnp.abs(distance)).astype(BF16)

    strip_rows = 32

    def render(e):
        spots = [e * capacity + c for c in range(capacity)]
        for c in range(capacity):
            for k in range(layers):
                across = interp(spacing[...] - shift_s[spots[c], 3 * k])
                downward_t = interp(spacing[...] + shift_s[spots[c], 3 * k + 1])
                halfway = jnp.dot(across, recv_buf[e, c, k], preferred_element_type=F32).astype(BF16)
                dense[c, k] = jnp.dot(halfway, downward_t, preferred_element_type=F32)
        for c in range(capacity):
            for begin in range(0, extent, strip_rows):
                lines = slice(begin, begin + strip_rows)
                optical, clear, colors = None, None, [None] * 3
                for k in range(layers):
                    density = dense[c, k, lines, :]
                    rate = shift_s[spots[c], 3 * k + 2]
                    soft = jnp.maximum(density, 0.0) + jnp.log(1.0 + jnp.exp(-jnp.abs(density)))
                    thickness = rate * soft
                    passed = jnp.exp(-thickness)
                    half_alpha = 0.5 - 0.5 * passed
                    if k:
                        half_alpha = half_alpha * clear
                    for n in range(3):
                        lit = half_alpha + half_alpha * jnp.tanh(
                            (0.5 * gain[n]) * density + 0.5 * bias[n]
                        )
                        colors[n] = lit if k == 0 else colors[n] + lit
                    optical = thickness if k == 0 else optical + thickness
                    clear = passed if k == 0 else clear * passed
                for n in range(3):
                    foot[spots[c], n, lines, :] = colors[n].astype(BF16)
                foot[spots[c], 3, lines, :] = optical.astype(BF16)

    for d in range(nz):
        below = exists(0, d)
        number = jnp.int32(1) if d == 0 else below.astype(jnp.int32) + exists(1, d).astype(jnp.int32)

        def entry(i, _):
            if d + 1 < whole:
                for way in range(2):
                    @pl.when(exists(way, d + 1) & (i < pieces))
                    def _():
                        block_copy(way, d, i).wait_recv()
                        if d + 2 < whole:
                            offer(way, d + 1, i)

                @pl.when(i == pieces - 1)
                def _():
                    for way in range(2):
                        if d + 2 == whole and whole < nz:
                            @pl.when(exists(way, d + 1) & has_next[way])
                            def _():
                                far(way)

                    for way in range(2):
                        @pl.when(exists(way, d + 1))
                        def _():
                            dz = step_of(way, d + 1)
                            for dy in range(1, ny):
                                share(held(way, d + 1), column_s.at[dz, 0], dz, dy)
                            gather(held(way, d + 1), column_s.at[dz, 0], my_y, my_z, recv_buf, dz * ny)

            dz = jnp.where((i < ny) & below, d, nz - d)
            e = dz * ny + lax.rem(i, ny)

            @pl.when((lax.rem(i, ny) > 0) | (d >= whole))
            def _():
                brick_copy(e, my_y, my_z).wait_recv()

            render(e)
            return 0

        lax.fori_loop(0, number * ny, entry, 0)

    def left(e, _):
        table_copy(e, my_y, my_z).wait_send()

        sent = lax.rem(e, ny) > 0
        if whole < nz:
            dz = lax.div(e, ny)
            first, last = (my_z == 0) & (dz == 1), (my_z == nz - 1) & (dz == nz - 1)
            sent = sent & jnp.logical_not(first | last)

        @pl.when(sent)
        def _():
            brick_copy(e, my_y, my_z).wait_send()

        return 0

    lax.fori_loop(1, row, left, 0)
    for dz in range(1, nz):
        column_copy(dz, my_z).wait_send()
    for way in range(2):
        for d in range(whole - 1):
            @pl.when(exists(way, d) & has_next[way])
            def _():
                for j in range(pieces):
                    block_copy(way, d, j).wait_send()
        if whole < nz:
            @pl.when(exists(way, whole - 1) & has_next[way])
            def _():
                for dy in range(ny):
                    far_copy(way, dy, my_y).wait_send()

    height = 16

    def strip(r, _):
        lines = pl.ds(pl.multiple_of(r * height, height), height)

        def visit(p, carry):
            optical0, optical1, color0, color1 = carry
            which = sort_s[0, p]
            in0 = sort_s[1, p].astype(F32)
            in1 = sort_s[2, p].astype(F32)
            clear = jnp.exp(-(optical0 * in0 + optical1 * in1))
            clear0, clear1 = clear * in0, clear * in1
            shade = [foot[which, n, lines, :].astype(F32) for n in range(3)]
            depth = foot[which, 3, lines, :].astype(F32)
            return (
                optical0 + in0 * depth,
                optical1 + in1 * depth,
                tuple(c + clear0 * s for c, s in zip(color0, shade)),
                tuple(c + clear1 * s for c, s in zip(color1, shade)),
            )

        zero = jnp.zeros((height, extent), F32)
        optical0, optical1, color0, color1 = lax.fori_loop(
            0, slots, visit, (zero, zero, (zero,) * 3, (zero,) * 3), unroll=8
        )
        for n in range(3):
            out[0, n, lines, :] = color0[n]
            out[1, n, lines, :] = color1[n]
        out[0, 3, lines, :] = jnp.exp(-optical0)
        out[1, 3, lines, :] = jnp.exp(-optical1)
        return 0

    lax.fori_loop(0, extent // height, strip, 0)


def body(ny, nz, bricks, live, shear, offsets, absorb, color_gain, color_bias, targets, order):
    brick_count, layers, extent, _ = bricks.shape
    views = targets.shape[1]
    row = ny * nz
    capacity = (brick_count * views + row - 1) // row
    slots = row * capacity
    smem = pl.BlockSpec(memory_space=pltpu.SMEM)
    vmem = pl.BlockSpec(memory_space=pltpu.VMEM)
    hbm = pl.BlockSpec(memory_space=pltpu.HBM)
    shear, offsets, targets = shear.T, offsets.transpose(1, 2, 0), targets.T
    live_row, absorb_row = live.reshape(1, brick_count), absorb.reshape(1, brick_count)
    table_rows = (capacity + 7) // 8 * 8
    longest = max(slots, brick_count * views)
    size = (longest + LANES - 1) // LANES * LANES
    return pl.pallas_call(
        functools.partial(main_kernel, ny, nz, capacity),
        out_shape=jax.ShapeDtypeStruct((2, 4, extent, extent), F32),
        in_specs=[hbm, hbm, hbm, hbm, hbm, smem, smem, hbm, hbm],
        out_specs=vmem,
        scratch_shapes=[
            pltpu.VMEM(bricks.shape, BF16),
            pltpu.VMEM((nz, 8, size), jnp.int32),
            pltpu.SMEM((nz, 8, size), jnp.int32),
            pltpu.VMEM((row, capacity, layers, extent, extent), BF16),
            pltpu.VMEM((row, capacity, layers, extent, extent), BF16),
            pltpu.VMEM((row, table_rows, LANES), jnp.int32),
            pltpu.VMEM((row, table_rows, LANES), jnp.int32),
            pltpu.VMEM((LANES, LANES), jnp.int32),
            pltpu.VMEM((size, LANES), jnp.int32),
            pltpu.VMEM((8, size), jnp.int32),
            pltpu.SMEM((8, size), jnp.int32),
            pltpu.VMEM((size, LANES), F32),
            pltpu.SMEM((size, LANES), F32),
            pltpu.VMEM((8, size), jnp.int32),
            pltpu.SMEM((8, size), jnp.int32),
            pltpu.VMEM((extent, extent), F32),
            pltpu.VMEM((capacity, layers, extent, extent), F32),
            pltpu.VMEM((slots, 4, extent, extent), BF16),
            pltpu.VMEM((size, LANES), jnp.int32),
            pltpu.SemaphoreType.DMA((row,)),
            pltpu.SemaphoreType.DMA((row,)),
            pltpu.SemaphoreType.DMA((row,)),
            pltpu.SemaphoreType.DMA((row,)),
            pltpu.SemaphoreType.DMA((nz,)),
            pltpu.SemaphoreType.DMA((nz,)),
            pltpu.SemaphoreType.DMA((2 * nz * ny,)),
            pltpu.SemaphoreType.DMA((2 * nz * ny,)),
            pltpu.VMEM((2 * ny, capacity, layers, extent, extent), BF16),
            pltpu.SemaphoreType.DMA((2 * ny,)),
            pltpu.SemaphoreType.DMA((11,)),
            *[
                pltpu.VMEM(a.shape, a.dtype)
                for a in (live_row, shear, offsets, absorb_row, targets, order)
            ],
            *[pltpu.VMEM(bricks.shape, BF16) for _ in range(2 * (nz - 1))],
        ],
        compiler_params=pltpu.CompilerParams(
            collective_id=0, has_side_effects=True, vmem_limit_bytes=60 * 1024 * 1024
        ),
    )(
        bricks, live_row, shear, offsets, absorb_row,
        color_gain, color_bias, targets, order,
    )


def solution(mesh):
    ny, nz = mesh.shape["gy"], mesh.shape["gz"]
    split = ("gx", "gy", "gz")
    placed = (
        P(split, None, None, None),
        P(split),
        P(),
        P(split, None, None),
        P(split),
        P(),
        P(),
        P(split, None),
        P(None, split),
    )
    return jax.shard_map(
        functools.partial(body, ny, nz),
        mesh=mesh,
        in_specs=placed,
        out_specs=P(split, None, None, None),
        check_vma=False,
    )
```
